256 devices in a mesh: dp: 16 (over z, x_hi), tensor: 16 (over x_lo, y, core).
Axes of the slice: x: 4 (x_hi: 2, x_lo: 2; x = x_hi * 2 + x_lo), y: 4, z: 8, core: 2. Of those that a mesh axis runs over, the one named last changes fastest.
Arguments:
- tokens: bfloat16 [256, 16384], P('dp'), may hold values from -6 to 6
- gate_codes: bfloat16 [16384, 26624], P('dp', 'tensor'), may hold values from 0 to 255, as said below
- gate_scales: bfloat16 [128, 53248], P('dp', 'tensor'), may hold values from 0.00077819824 to 0.003112793
- up_codes: bfloat16 [16384, 26624], P('dp', 'tensor'), may hold values from 0 to 255, as said below
- up_scales: bfloat16 [128, 53248], P('dp', 'tensor'), may hold values from 0.00077819824 to 0.003112793
- down_codes: bfloat16 [53248, 8192], P('tensor', 'dp'), may hold values from 0 to 255, as said below
- down_scales: bfloat16 [416, 16384], P('tensor', 'dp'), may hold values from 0.00043296814 to 0.0017318726
- sign_bits: int32 [3328, 208], P('dp'), may hold values from 0 to 65535
Outputs:
- mixed: bfloat16 [256, 16384], P('tensor', 'dp')
- token_absmax: float32 [256], P('dp')
The draws below stay inside these ranges and needn't reach their ends.
Inputs may be any that keep to these rules, and one draw needn't show every extreme that they name: `gate_codes`: whole numbers; entry w of a row holds the codes of columns 2 w (low four bits) and 2 w + 1 (high four bits); every bit is random. `up_codes`: same layout as gate_codes. `down_codes`: same layout as gate_codes, over the columns of the model width. `sign_bits`: bit k of word w in row a is the sign bit of column 16 w + k; every bit is random.
All inputs are finite; a program needn't handle non-finite values.
Results may differ from the reference program's by a relative error of at most 0.039.
Values may be sent and summed in bfloat16 or wider, within the bound.
A program may use at most 128 MiB of HBM per device.

```python
import math
import jax
import jax.numpy as jnp
from jax import lax

D = 16384
FF = 53248
GROUP = 128
TOKENS = 256
HB = 3328
N_DP = 16
N_TENSOR = 16


def draw_gate_codes(key, part):
    key = jax.random.fold_in(key, 11)
    return jax.random.randint(key, (D, FF // 2), 0, 256).astype(jnp.float32).astype(jnp.bfloat16)


def draw_up_codes(key, part):
    key = jax.random.fold_in(key, 23)
    return jax.random.randint(key, (D, FF // 2), 0, 256).astype(jnp.float32).astype(jnp.bfloat16)


def draw_down_codes(key, part):
    key = jax.random.fold_in(key, 37)
    return jax.random.randint(key, (FF, D // 2), 0, 256).astype(jnp.float32).astype(jnp.bfloat16)


def touch_ends(values, rng, smallest, high):
    longest = values.shape.index(max(values.shape))
    spots = []
    for shift in (0, 1):
        where = [jax.random.randint(jax.random.fold_in(rng, axis), (), 0, length) for axis, length in enumerate(values.shape)]
        where[longest] = (where[longest] + shift) % values.shape[longest]
        spots.append(tuple(where))
    return values.at[spots[0]].set(smallest).at[spots[1]].set(high)


def shard_levels(rng, shape, pieces, smallest, top_value):
    loudness = 1.0
    for dim, blocks in pieces:
        heights = jax.random.uniform(jax.random.fold_in(jax.random.fold_in(rng, 6), dim), (blocks,), jnp.float32, smallest / len(pieces), top_value / len(pieces))
        loudness = loudness * jnp.repeat(jnp.exp(heights), shape[dim] // blocks).reshape((-1,) + (1,) * (len(shape) - 1 - dim))
    return loudness


def noise(rng, shape, width, bound, split=(), held_as=jnp.bfloat16):
    entries = width * jax.random.normal(rng, shape, jnp.float32)
    if split:
        entries = entries * shard_levels(rng, shape, split, -0.22, 0.18)
    return jnp.clip(entries, -bound, bound).astype(held_as)


def setup_inputs(seed: int = 0) -> dict:
    streams_of = jax.random.split(jax.random.key(seed), 9)
    return {
        "tokens": noise(streams_of[0], (TOKENS, D), 1.0, 6.0, ((0, 16),)),
        "gate_codes": draw_gate_codes(jax.random.fold_in(streams_of[8], 71), 0),
        "gate_scales": jnp.clip(jnp.exp(math.log(0.003112793) - 1.3862944 * jax.random.uniform(streams_of[2], (D // GROUP, FF), jnp.float32) ** shard_levels(streams_of[2], (D // GROUP, FF), ((0, 16), (1, 16)), -0.2, 0.2)), 0.00077819824, 0.003112793).astype(jnp.bfloat16),
        "up_codes": draw_up_codes(jax.random.fold_in(streams_of[8], 71), 0),
        "up_scales": jnp.clip(jnp.exp(math.log(0.003112793) - 1.3862944 * jax.random.uniform(streams_of[4], (D // GROUP, FF), jnp.float32) ** shard_levels(streams_of[4], (D // GROUP, FF), ((0, 16), (1, 16)), -0.2, 0.2)), 0.00077819824, 0.003112793).astype(jnp.bfloat16),
        "down_codes": draw_down_codes(jax.random.fold_in(streams_of[8], 71), 0),
        "down_scales": jnp.clip(jnp.exp(math.log(0.0017318726) - 1.3862944 * jax.random.uniform(streams_of[6], (FF // GROUP, D), jnp.float32) ** shard_levels(streams_of[6], (FF // GROUP, D), ((0, 16), (1, 16)), -0.2, 0.2)), 0.00043296814, 0.0017318726).astype(jnp.bfloat16),
        "sign_bits": touch_ends(jax.random.randint(streams_of[7], (HB, HB // 16), 0, 65536), jax.random.fold_in(streams_of[7], 1), 0, 65535).astype(jnp.int32),
    }


def dequant(packed, scales, group_size):
    row_count, word_count = packed.shape
    scale_grid = scales.astype(jnp.float32).reshape(row_count // group_size, 1, word_count, 2)
    whole = packed.astype(jnp.int32).reshape(row_count // group_size, group_size, word_count, 1)
    shifts = jnp.array([0, 4], jnp.int32).reshape(1, 1, 1, 2)
    code_vals = jnp.bitwise_and(jnp.right_shift(whole, shifts), 15) - 8
    values = (code_vals.astype(jnp.float32) * scale_grid).astype(jnp.bfloat16)
    return values.reshape(row_count, word_count * 2)

def unpack_signs(sign_bits):
    row_count, word_count = sign_bits.shape
    shifts = jnp.arange(16, dtype=jnp.int32).reshape(1, 1, 16)
    flag = jnp.bitwise_and(jnp.right_shift(sign_bits[:, :, None], shifts), 1)
    return (1 - 2 * flag).astype(jnp.bfloat16).reshape(row_count, word_count * 16)

def walsh(order):
    first = jnp.arange(order, dtype=jnp.int32)[:, None]
    second = jnp.arange(order, dtype=jnp.int32)[None, :]
    parity = jnp.zeros((order, order), jnp.int32)
    for bit_pos in range(order.bit_length() - 1):
        parity = parity + jnp.bitwise_and(jnp.right_shift(first, bit_pos), 1) * jnp.bitwise_and(jnp.right_shift(second, bit_pos), 1)
    return (1 - 2 * (parity % 2)).astype(jnp.float32)

def reference(tokens, gate_codes, gate_scales, up_codes, up_scales, down_codes, down_scales, sign_bits):
    block_hidden = FF // N_TENSOR
    block_model = D // N_DP
    signs = unpack_signs(sign_bits)
    zero_index = jnp.zeros((), jnp.int32)

    def hidden_block(block_index):
        block_index = block_index.astype(jnp.int32)
        col_word = (block_index * (block_hidden // 2)).astype(jnp.int32)
        column = (block_index * block_hidden).astype(jnp.int32)

        def add_term(carry, row_index):
            row_index = row_index.astype(jnp.int32)
            first_row = (row_index * block_model).astype(jnp.int32)
            group_row = (row_index * (block_model // GROUP)).astype(jnp.int32)
            left = lax.dynamic_slice_in_dim(tokens, first_row, block_model, 1)
            gate_dense = dequant(lax.dynamic_slice(gate_codes, (first_row, col_word), (block_model, block_hidden // 2)), lax.dynamic_slice(gate_scales, (group_row, column), (block_model // GROUP, block_hidden)), GROUP)
            up_dense = dequant(lax.dynamic_slice(up_codes, (first_row, col_word), (block_model, block_hidden // 2)), lax.dynamic_slice(up_scales, (group_row, column), (block_model // GROUP, block_hidden)), GROUP)
            term = jnp.concatenate([jnp.dot(left, gate_dense, preferred_element_type=jnp.float32), jnp.dot(left, up_dense, preferred_element_type=jnp.float32)], axis=1).astype(jnp.bfloat16)
            term = lax.optimization_barrier(term)
            return (carry + term.astype(jnp.float32), None)
        start_sum = jnp.zeros((tokens.shape[0], 2 * block_hidden), jnp.float32)
        total, _ = lax.scan(add_term, start_sum, jnp.arange(N_DP, dtype=jnp.int32))
        gate_sum = total[:, :block_hidden]
        up_sum = total[:, block_hidden:]
        hidden = (jax.nn.silu(gate_sum) * up_sum).astype(jnp.bfloat16)
        return lax.dot_general(hidden, signs, (((1,), (1,)), ((), ())), preferred_element_type=jnp.float32)
    turned = lax.map(hidden_block, jnp.arange(N_TENSOR, dtype=jnp.int32))
    mixer = walsh(N_TENSOR)
    rotated = jnp.einsum('ab,btk->atk', mixer, turned, precision=lax.Precision.HIGHEST) * (1.0 / math.sqrt(FF))
    rotated = rotated.astype(jnp.bfloat16)
    token_absmax = lax.optimization_barrier(jnp.max(jnp.abs(rotated.astype(jnp.float32)), axis=(0, 2)))

    def add_down(carry, pair):
        rotated_block, block_index = pair
        block_index = block_index.astype(jnp.int32)
        code_row = (block_index * block_hidden).astype(jnp.int32)
        scale_row = (block_index * (block_hidden // GROUP)).astype(jnp.int32)
        down_dense = dequant(lax.dynamic_slice(down_codes, (code_row, zero_index), (block_hidden, D // 2)), lax.dynamic_slice(down_scales, (scale_row, zero_index), (block_hidden // GROUP, D)), GROUP)
        return (carry + jnp.dot(rotated_block, down_dense, preferred_element_type=jnp.float32), None)
    start_out = jnp.zeros((tokens.shape[0], D), jnp.float32)
    output, _ = lax.scan(add_down, start_out, (rotated, jnp.arange(N_TENSOR, dtype=jnp.int32)))
    return (output.astype(jnp.bfloat16), token_absmax)
```

```python
import math

import jax
import jax.numpy as jnp
from jax import lax
from jax.experimental import pallas as pl
from jax.experimental.pallas import tpu as pltpu
from jax.sharding import PartitionSpec as P

FF = 53248
HB = 3328
NB = 13
NDP = 16
NT = 16
MESH = pl.DeviceIdType.MESH
BF = jnp.bfloat16
F32 = jnp.float32

LAG_Z = 2
LAG_H = 4
LAG_W = 5
LAG_G = 6
LAG_X = 8
LAG_S = 10
LAG_U = 5
TICKS = NB + LAG_S
NOUT = 2


def eo_column(p):
    return jnp.where(p < 128, 2 * p, 2 * (p - 128) + 1)


def one_hot(cond):
    return jnp.where(cond, 1.0, 0.0).astype(BF)


def body(tokens, gc, gs, uc, us, dc, ds, sb, out, peak,
         x, gcv, ucv, dcv, own, xr, zr, hs, w1r, v, g, sw, st, dw, racc, rot, es, er, pk, pr,
         gsv, usv, dsv, sbp, sbt, wb, perm_in, perm_h, perm_out, walsh,
         code_sem, dcode_sem, loc_sem, a_send, a_recv, sib_sem, s1_send, s1_recv, s2_send, s2_recv,
         x_send, x_recv, z_send, z_recv, w1_send, w1_recv, w2_send, w2_recv, g_send, g_recv,
         gx_send, gx_recv, e_send, e_recv, p_send, p_recv):
    d = lax.axis_index("dp")
    t = lax.axis_index("tensor")
    core = lax.rem(t, 2)
    s = lax.rem(t, 8)
    z = d // 2
    xh = lax.rem(d, 2)
    row = xh * 8 + z
    partner = z * 2 + (1 - xh)

    def place(dp):
        return lax.rem(dp, 2) * 8 + dp // 2

    def remote(src, dst, ssem, rsem, dp, tn):
        return pltpu.make_async_remote_copy(
            src_ref=src, dst_ref=dst, send_sem=ssem, recv_sem=rsem, device_id=(dp, tn), device_id_type=MESH)

    def wait_bytes(ref, sem):
        pltpu.make_async_copy(ref, ref, sem).wait()

    def code_copies(c):
        lanes = pl.ds(pl.multiple_of(c * 128, 128), 128)
        return (pltpu.make_async_copy(gc.at[:, lanes], gcv.at[c], code_sem.at[0, c]),
                pltpu.make_async_copy(uc.at[:, lanes], ucv.at[c], code_sem.at[1, c]))

    def start_codes(c, carry):
        for copy in code_copies(c):
            copy.start()
        return carry

    lax.fori_loop(0, NB, start_codes, 0)
    dcopy = pltpu.make_async_copy(dc, dcv, dcode_sem)
    dcopy.start()

    barrier = pltpu.get_barrier_semaphore()

    def greet(j, carry):
        pl.semaphore_signal(barrier, inc=1, device_id=(lax.rem(d + j, NDP), t), device_id_type=MESH)
        pl.semaphore_signal(barrier, inc=1, device_id=(d, lax.rem(t + j, NT)), device_id_type=MESH)
        return carry

    lax.fori_loop(1, NDP, greet, 0)

    sbp[...] = jnp.zeros_like(sbp)
    sbp[0:208, 0:208] = sb[...]
    sbt[...] = jnp.transpose(sbp[...]).reshape(16, 16, 256)

    @pl.when(s < 7)
    def _():
        for u in range(2):
            sw[2 * s + u, d] = sbt[2 * s + u].astype(jnp.int16)

    pl.semaphore_wait(barrier, 2 * (NDP - 1))

    def token_copy(dst_dp):
        lanes = pl.ds(pl.multiple_of(dst_dp * 1024 + core * 512, 512), 512)
        return tokens.at[:, lanes]

    def send_tokens(j, carry):
        to = lax.rem(d + j, NDP)
        remote(token_copy(to), x.at[core, row], a_send, a_recv, to, t).start()
        return carry

    lax.fori_loop(1, NDP, send_tokens, 0)
    mine = pltpu.make_async_copy(token_copy(d), x.at[core, row], loc_sem)
    mine.start()

    @pl.when(s < 7)
    def _():
        def send_words(j, carry):
            part = sw.at[pl.ds(2 * s, 2), d]
            remote(part, part, s1_send, s1_recv, lax.rem(d + j, NDP), t).start()
            return carry

        lax.fori_loop(1, NDP, send_words, 0)

    src = lax.broadcasted_iota(jnp.int32, (256, 256), 0)
    dst = lax.broadcasted_iota(jnp.int32, (256, 256), 1)
    perm_in[...] = one_hot(src == eo_column(dst))
    perm_out[...] = one_hot(dst == eo_column(src))
    perm_h[...] = one_hot(eo_column(src) == 16 * (dst & 15) + (dst >> 4))
    both = (src >> 4) & (dst >> 4)
    odd = (both ^ (both >> 1) ^ (both >> 2) ^ (both >> 3)) & 1
    walsh[...] = jnp.where((src & 15) == (dst & 15), jnp.where(odd == 1, -1.0, 1.0), 0.0).astype(BF)

    for b in range(NB):
        cols = slice(256 * b, 256 * b + 256)
        gsv[b] = jnp.dot(gs[:, cols], perm_in[...], preferred_element_type=F32)
        usv[b] = jnp.dot(us[:, cols], perm_in[...], preferred_element_type=F32)
    for n in range(4):
        cols = slice(256 * n, 256 * n + 256)
        dsv[:, cols] = jnp.dot(ds[:, cols], perm_in[...], preferred_element_type=F32)

    wait_bytes(x.at[core, pl.ds(0, NDP - 1)], a_recv)
    mine.wait()
    sib = remote(x.at[core], x.at[core], sib_sem.at[0], sib_sem.at[1], d, t + 1 - 2 * core)
    sib.start()
    sib.wait_recv()

    def nibbles(codes):
        whole = codes.astype(F32)
        high = jnp.floor(whole * 0.0625)
        return whole - 16.0 * high - 8.0, high - 8.0

    def gate_up(c):
        for copy in code_copies(c):
            copy.wait()
        for base, codes, scales in ((0, gcv, gsv), (256, ucv, usv)):
            for r in range(8):
                rows = slice(128 * r, 128 * r + 128)
                low, high = nibbles(codes[c, rows, :])
                sc = scales[c, r:r + 1, :]
                wb[rows, base:base + 128] = (low * sc[:, 0:128]).astype(BF)
                wb[rows, base + 128:base + 256] = (high * sc[:, 128:256]).astype(BF)
        part = jnp.dot(x[0].reshape(256, 512), wb[0:512, :], preferred_element_type=F32)
        part = part + jnp.dot(x[1].reshape(256, 512), wb[512:1024, :], preferred_element_type=F32)
        own[c] = part.astype(BF).reshape(16, 16, 512)
        remote(own.at[c, pl.ds((1 - xh) * 8, 8)], xr.at[c], x_send, x_recv.at[c], partner, t).start()

    def down_weights(b):
        @pl.when(b == 0)
        def _():
            dcopy.wait()

        for r in range(2):
            rows = pl.ds(pl.multiple_of(256 * b + 128 * r, 128), 128)
            low, high = nibbles(dcv[rows, :])
            sc = dsv[pl.ds(2 * b + r, 1), :]
            for n in range(4):
                words = slice(128 * n, 128 * n + 128)
                dw[rows, 256 * n:256 * n + 128] = (low[:, words] * sc[:, 256 * n:256 * n + 128]).astype(BF)
                dw[rows, 256 * n + 128:256 * n + 256] = (high[:, words] * sc[:, 256 * n + 128:256 * n + 256]).astype(BF)

    def share_words():
        @pl.when(s < 7)
        def _():
            wait_bytes(sw.at[pl.ds(0, 2), pl.ds(0, NDP - 1)], s1_recv)

            def send(j, carry):
                to = t - s + lax.rem(s + j, 8)
                part = sw.at[pl.ds(2 * s, 2)]
                remote(part, part, s2_send, s2_recv.at[s], d, to).start()
                return carry

            lax.fori_loop(1, 8, send, 0)

    def wait_words():
        for q in range(7):
            @pl.when(s != q)
            def _():
                wait_bytes(sw.at[pl.ds(2 * q, 2)], s2_recv.at[q])

    def unpack(b):
        words = jnp.concatenate([sw[b, q].astype(jnp.int32)[:, 0:208] for q in range(NDP)], axis=1)
        for k in range(16):
            st[b, 16 * k:16 * k + 16, :] = jnp.where((words & (1 << k)) == 0, 1.0, -1.0).astype(BF)

    def z_phase(c):
        wait_bytes(xr.at[c], x_recv.at[c])
        half = pl.ds(xh * 8, 8)
        own[c, half] = (own[c, half].astype(F32) + xr[c].astype(F32)).astype(BF)

        def send(j, carry):
            zz = lax.rem(z + j, 8)
            remote(own.at[c, xh * 8 + zz], zr.at[c, j - 1], z_send, z_recv.at[c], zz * 2 + xh, t).start()
            return carry

        lax.fori_loop(1, 8, send, 0)

    def hidden(c):
        wait_bytes(zr.at[c], z_recv.at[c])
        total = own[c, row].astype(F32)
        for j in range(7):
            total = total + zr[c, j].astype(F32)
        gate, up = total[:, 0:256], total[:, 256:512]
        hs[c] = (gate / (1.0 + jnp.exp(-gate)) * up).astype(BF)

        @pl.when(t == c)
        def _():
            w1r[t] = hs[c]

        @pl.when(t != c)
        def _():
            remote(hs.at[c], w1r.at[t], w1_send, w1_recv, d, c).start()

    def mix(c):
        @pl.when(t == c)
        def _():
            wait_bytes(w1r.at[pl.ds(0, NT - 1)], w1_recv)
            turned = jnp.dot(w1r[...].reshape(256, 256), perm_h[...], preferred_element_type=F32).astype(BF)
            mixed = jnp.dot(walsh[...], turned, preferred_element_type=F32) * (1.0 / math.sqrt(FF))
            v[...] = mixed.astype(BF).reshape(16, 16, 256)
            g[c, row] = v[t]

            def send(j, carry):
                to = lax.rem(t + j, NT)
                remote(v.at[to], g.at[c, row], w2_send, w2_recv.at[c], d, to).start()
                return carry

            lax.fori_loop(1, NT, send, 0)

    def gather_z(b):
        @pl.when(t != b)
        def _():
            wait_bytes(g.at[b, row], w2_recv.at[b])

        def send(j, carry):
            zz = lax.rem(z + j, 8)
            remote(g.at[b, row], g.at[b, row], g_send, g_recv.at[b], zz * 2 + xh, t).start()
            return carry

        lax.fori_loop(1, 8, send, 0)

    def gather_x(b):
        wait_bytes(g.at[b, pl.ds(xh * 8, 7)], g_recv.at[b])
        half = g.at[b, pl.ds(xh * 8, 8)]
        remote(half, half, gx_send, gx_recv.at[b], partner, t).start()

    def turn(b):
        wait_bytes(g.at[b, pl.ds((1 - xh) * 8, 8)], gx_recv.at[b])
        left = g[b].reshape(256, 256)
        for n in range(NB):
            cols = slice(256 * n, 256 * n + 256)
            racc[:, cols] += jnp.dot(left, st[b, :, cols], preferred_element_type=F32)

    def during(i, lag, stage):
        @pl.when((i >= lag) & (i < NB + lag))
        def _():
            stage(i - lag)

    racc[...] = jnp.zeros_like(racc)

    def tick(i, carry):
        during(i, 0, gate_up)
        during(i, LAG_Z, z_phase)
        during(i, LAG_H, hidden)
        during(i, LAG_W, mix)
        during(i, LAG_G, gather_z)
        during(i, LAG_X, gather_x)

        @pl.when(i == 1)
        def _():
            share_words()

        during(i, 1, down_weights)

        @pl.when(i == LAG_U)
        def _():
            wait_words()

        during(i, LAG_U, unpack)
        during(i, LAG_S, turn)
        return carry

    lax.fori_loop(0, TICKS, tick, 0)

    rot[...] = racc[...].astype(BF).reshape(16, 16, HB)
    top = jnp.max(jnp.abs(rot[row].astype(F32)), axis=1, keepdims=True)
    pk[...] = jnp.broadcast_to(top, (16, 128))
    pr[t] = pk[...]

    def send_peak(j, carry):
        remote(pk, pr.at[t], p_send, p_recv, d, lax.rem(t + j, NT)).start()
        return carry

    lax.fori_loop(1, NT, send_peak, 0)

    width = 1024 // NOUT
    for n in range(NOUT):
        cols = slice(width * n, width * n + width)
        part = jnp.dot(rot[...].reshape(256, HB), dw[:, cols], preferred_element_type=F32)
        es[n] = part.astype(BF).reshape(16, 16, width)
        er[n, t] = es[n, place(t)]

        def send_out(j, carry, n=n):
            to = lax.rem(t + j, NT)
            remote(es.at[n, place(to)], er.at[n, t], e_send.at[n], e_recv.at[n], d, to).start()
            return carry

        lax.fori_loop(1, NT, send_out, 0)

    wait_bytes(pr.at[pl.ds(0, NT - 1)], p_recv)
    high = pr[0]
    for q in range(1, NT):
        high = jnp.maximum(high, pr[q])
    peak[...] = jnp.transpose(high)[0:1, :]

    for n in range(NOUT):
        wait_bytes(er.at[n, pl.ds(0, NT - 1)], e_recv.at[n])
        total = er[n, 0].astype(F32)
        for q in range(1, NT):
            total = total + er[n, q].astype(F32)
        total = total.astype(BF)
        for m in range(width // 256):
            lo = width * n + 256 * m
            out[:, lo:lo + 256] = jnp.dot(
                total[:, 256 * m:256 * m + 256], perm_out[...], preferred_element_type=F32).astype(BF)

    wait_bytes(x.at[core, pl.ds(0, NDP - 1)], a_send)
    sib.wait_send()

    @pl.when(s < 7)
    def _():
        wait_bytes(sw.at[pl.ds(0, 2), pl.ds(0, NDP - 1)], s1_send)
        wait_bytes(sw, s2_send)

    wait_bytes(xr, x_send)
    wait_bytes(zr, z_send)

    @pl.when(t < NB)
    def _():
        wait_bytes(hs.at[pl.ds(0, NB - 1)], w1_send)
        wait_bytes(v.at[pl.ds(0, NT - 1)], w2_send)

    @pl.when(t >= NB)
    def _():
        wait_bytes(hs, w1_send)

    wait_bytes(g.at[:, pl.ds(0, 7)], g_send)
    wait_bytes(g.at[:, pl.ds(0, 8)], gx_send)
    for n in range(NOUT):
        wait_bytes(es.at[n, pl.ds(0, NT - 1)], e_send.at[n])
    wait_bytes(pr.at[pl.ds(0, NT - 1)], p_send)


def local(tokens, gc, gs, uc, us, dc, ds, sb):
    dma = pltpu.SemaphoreType.DMA
    vm = pltpu.VMEM
    any_spec = pl.BlockSpec(memory_space=pl.ANY)
    vm_spec = pl.BlockSpec(memory_space=pltpu.VMEM)
    width = 1024 // NOUT
    out, peak = pl.pallas_call(
        body,
        out_shape=(jax.ShapeDtypeStruct((16, 1024), BF), jax.ShapeDtypeStruct((1, 16), F32)),
        in_specs=[any_spec, any_spec, vm_spec, any_spec, vm_spec, any_spec, vm_spec, vm_spec],
        out_specs=(vm_spec, vm_spec),
        scratch_shapes=[
            vm((2, 16, 16, 512), BF),
            vm((NB, 1024, 128), BF),
            vm((NB, 1024, 128), BF),
            vm((HB, 512), BF),
            vm((NB, 16, 16, 512), BF),
            vm((NB, 8, 16, 512), BF),
            vm((NB, 7, 16, 512), BF),
            vm((NB, 16, 256), BF),
            vm((16, 16, 256), BF),
            vm((16, 16, 256), BF),
            vm((NB, 16, 16, 256), BF),
            vm((14, 16, 16, 256), jnp.int16),
            vm((NB, 256, HB), BF),
            vm((HB, 1024), BF),
            vm((256, HB), F32),
            vm((16, 16, HB), BF),
            vm((NOUT, 16, 16, width), BF),
            vm((NOUT, 16, 16, width), BF),
            vm((16, 128), F32),
            vm((16, 16, 128), F32),
            vm((NB, 8, 256), F32),
            vm((NB, 8, 256), F32),
            vm((26, 1024), F32),
            vm((256, 256), jnp.int32),
            vm((16, 16, 256), jnp.int32),
            vm((1024, 512), BF),
            vm((256, 256), BF),
            vm((256, 256), BF),
            vm((256, 256), BF),
            vm((256, 256), BF),
            dma((2, NB)), dma, dma, dma, dma, dma((2,)), dma, dma, dma, dma((8,)),
            dma, dma((NB,)), dma, dma((NB,)), dma, dma, dma, dma((NB,)), dma, dma((NB,)),
            dma, dma((NB,)), dma((NOUT,)), dma((NOUT,)), dma, dma,
        ],
        compiler_params=pltpu.CompilerParams(
            collective_id=0, has_side_effects=True, vmem_limit_bytes=63 * 1024 * 1024),
    )(tokens, gc, gs, uc, us, dc, ds, sb)
    return out, peak.reshape(16)


def solution(mesh):
    return jax.shard_map(
        local,
        mesh=mesh,
        in_specs=(
            P("dp", None),
            P("dp", "tensor"),
            P("dp", "tensor"),
            P("dp", "tensor"),
            P("dp", "tensor"),
            P("tensor", "dp"),
            P("tensor", "dp"),
            P("dp", None),
        ),
        out_specs=(P("tensor", "dp"), P("dp")),
        check_vma=False,
    )
```

```python
import math

import jax
import jax.numpy as jnp
from jax import lax
from jax.experimental import pallas as pl
from jax.experimental.pallas import tpu as pltpu
from jax.sharding import PartitionSpec as P

FF = 53248
HB = 3328
NB = 13
NDP = 16
NT = 16
MESH = pl.DeviceIdType.MESH
BF = jnp.bfloat16
F32 = jnp.float32

NE = 9
ZEND = 5
NZF = (ZEND + 2) // 3
LAG_Z = (2, 2)
LAG_H = (6, 4)
LAG_W = (7, 5)
LAG_G = (8, 6)
LAG_X = (10, 8)
LAG_S = (12, 10)
TICKS = max(NE + LAG_S[0], NB + LAG_S[1])
T_SHARE = 2
T_SIBLING = 8
T_WORDS = min(LAG_S[0], NE + LAG_S[1])
NOUT = 2


def eo_column(p):
    return jnp.where(p < 128, 2 * p, 2 * (p - 128) + 1)


def one_hot(cond):
    return jnp.where(cond, 1.0, 0.0).astype(BF)


def body(tokens, gc, gs, uc, us, dc, ds, sb, out, peak,
         x, gcv, ucv, dcv, own, xr, zr, zr2, xr2, hs, w1r, v, g, sw, st, dw, racc, rot, es, er, pk, pr,
         gsv, usv, dsv, sbp, sbt, wb, perm_in, perm_h, perm_out, walsh,
         code_sem, dcode_sem, loc_sem, a_send, a_recv, sib_sem, s1_send, s1_recv, s2_send, s2_recv,
         s3_sem, x_send, x_recv, x2_send, x2_recv, z_send, z_recv, zz_send, zz_recv, w1_send, w1_recv, w2_send, w2_recv, g_send, g_recv,
         gx_send, gx_recv, e_send, e_recv, p_send, p_recv):
    d = lax.axis_index("dp")
    t = lax.axis_index("tensor")
    core = lax.rem(t, 2)
    y = lax.rem(t // 2, 4)
    s = core * 4 + y
    z = d // 2
    xh = lax.rem(d, 2)
    partner = z * 2 + (1 - xh)
    sibling = t + 1 - 2 * core

    def remote(src, dst, ssem, rsem, dp, tn):
        return pltpu.make_async_remote_copy(
            src_ref=src, dst_ref=dst, send_sem=ssem, recv_sem=rsem, device_id=(dp, tn), device_id_type=MESH)

    def wait_bytes(ref, sem):
        pltpu.make_async_copy(ref, ref, sem).wait()

    barrier = pltpu.get_barrier_semaphore()

    def greet(j, carry):
        pl.semaphore_signal(barrier, inc=1, device_id=(lax.rem(d + j, NDP), t), device_id_type=MESH)
        pl.semaphore_signal(barrier, inc=1, device_id=(d, lax.rem(t + j, NT)), device_id_type=MESH)
        return carry

    lax.fori_loop(1, NDP, greet, 0)

    def code_copies(c):
        lanes = pl.ds(pl.multiple_of(c * 128, 128), 128)
        return (pltpu.make_async_copy(gc.at[:, lanes], gcv.at[c], code_sem.at[0, c]),
                pltpu.make_async_copy(uc.at[:, lanes], ucv.at[c], code_sem.at[1, c]))

    def start_codes(c, carry):
        for copy in code_copies(c):
            copy.start()
        return carry

    lax.fori_loop(0, NB, start_codes, 0)
    dcopy = pltpu.make_async_copy(dc, dcv, dcode_sem)
    dcopy.start()

    sbp[...] = jnp.zeros_like(sbp)
    sbp[0:208, 0:208] = sb[...]
    sbt[...] = jnp.transpose(sbp[...]).reshape(16, 16, 256)

    @pl.when(s < 7)
    def _():
        for u in range(2):
            sw[2 * s + u, d] = sbt[2 * s + u].astype(jnp.int16)

    pl.semaphore_wait(barrier, 2 * (NDP - 1))

    def token_copy(dst_dp):
        lanes = pl.ds(pl.multiple_of(dst_dp * 1024 + core * 512, 512), 512)
        return tokens.at[:, lanes]

    def send_tokens(j, carry):
        to = lax.rem(d + j, NDP)
        remote(token_copy(to), x.at[core, d], a_send, a_recv, to, t).start()
        return carry

    lax.fori_loop(1, NDP, send_tokens, 0)
    mine = pltpu.make_async_copy(token_copy(d), x.at[core, d], loc_sem)
    mine.start()

    @pl.when(s < 7)
    def _():
        def send_words(j, carry):
            part = sw.at[pl.ds(2 * s, 2), d]
            remote(part, part, s1_send, s1_recv, lax.rem(d + j, NDP), t).start()
            return carry

        lax.fori_loop(1, NDP, send_words, 0)

    src = lax.broadcasted_iota(jnp.int32, (256, 256), 0)
    dst = lax.broadcasted_iota(jnp.int32, (256, 256), 1)
    perm_in[...] = one_hot(src == eo_column(dst))
    perm_out[...] = one_hot(dst == eo_column(src))
    perm_h[...] = one_hot(eo_column(src) == 16 * (dst & 15) + (dst >> 4))
    both = (src >> 4) & (dst >> 4)
    odd = (both ^ (both >> 1) ^ (both >> 2) ^ (both >> 3)) & 1
    walsh[...] = jnp.where((src & 15) == (dst & 15), jnp.where(odd == 1, -1.0, 1.0), 0.0).astype(BF)

    for b in range(NB):
        cols = slice(256 * b, 256 * b + 256)
        gsv[b] = jnp.dot(gs[:, cols], perm_in[...], preferred_element_type=F32)
        usv[b] = jnp.dot(us[:, cols], perm_in[...], preferred_element_type=F32)
    for n in range(4):
        cols = slice(256 * n, 256 * n + 256)
        dsv[:, cols] = jnp.dot(ds[:, cols], perm_in[...], preferred_element_type=F32)

    wait_bytes(x.at[core, pl.ds(0, NDP - 1)], a_recv)
    mine.wait()
    sib = remote(x.at[core], x.at[core], sib_sem.at[0], sib_sem.at[1], d, sibling)
    sib.start()
    sib.wait_recv()

    def nibbles(codes):
        whole = codes.astype(F32)
        high = jnp.floor(whole * 0.0625)
        return whole - 16.0 * high - 8.0, high - 8.0

    def gate_up(c):
        for copy in code_copies(c):
            copy.wait()
        for base, codes, scales in ((0, gcv, gsv), (256, ucv, usv)):
            for r in range(8):
                rows = slice(128 * r, 128 * r + 128)
                low, high = nibbles(codes[c, rows, :])
                sc = scales[c, r:r + 1, :]
                wb[rows, base:base + 128] = (low * sc[:, 0:128]).astype(BF)
                wb[rows, base + 128:base + 256] = (high * sc[:, 128:256]).astype(BF)
        part = jnp.dot(x[0].reshape(256, 512), wb[0:512, :], preferred_element_type=F32)
        part = part + jnp.dot(x[1].reshape(256, 512), wb[512:1024, :], preferred_element_type=F32)
        own[c] = part.astype(BF).reshape(8, 2, 16, 512)

        @pl.when(z_first(c))
        def _():
            chain(c, 1, True)

        @pl.when(jnp.logical_not(z_first(c)))
        def _():
            remote(own.at[c, :, 1 - xh], xr.at[c], x_send, x_recv.at[c], partner, t).start()

    def down_weights(b):
        @pl.when(b == 0)
        def _():
            dcopy.wait()

        for r in range(2):
            rows = pl.ds(pl.multiple_of(256 * b + 128 * r, 128), 128)
            low, high = nibbles(dcv[rows, :])
            sc = dsv[pl.ds(2 * b + r, 1), :]
            for n in range(4):
                words = slice(128 * n, 128 * n + 128)
                dw[rows, 256 * n:256 * n + 128] = (low[:, words] * sc[:, 256 * n:256 * n + 128]).astype(BF)
                dw[rows, 256 * n + 128:256 * n + 256] = (high[:, words] * sc[:, 256 * n + 128:256 * n + 256]).astype(BF)

    def share_words():
        @pl.when(s < 7)
        def _():
            wait_bytes(sw.at[pl.ds(0, 2), pl.ds(0, NDP - 1)], s1_recv)

            def send(j, carry):
                to = t + 2 * (lax.rem(y + j, 4) - y)
                part = sw.at[pl.ds(2 * s, 2)]
                remote(part, part, s2_send, s2_recv.at[y], d, to).start()
                return carry

            lax.fori_loop(1, 4, send, 0)

    def words_to_sibling():
        for q in range(4):
            @pl.when((y != q) & (core * 4 + q < 7))
            def _():
                wait_bytes(sw.at[pl.ds(2 * q, 2)], s2_recv.at[q])

        @pl.when(core == 0)
        def _():
            remote(sw.at[pl.ds(0, 8)], sw.at[pl.ds(0, 8)], s3_sem.at[0], s3_sem.at[1], d, sibling).start()

        @pl.when(core == 1)
        def _():
            remote(sw.at[pl.ds(8, 6)], sw.at[pl.ds(8, 6)], s3_sem.at[0], s3_sem.at[1], d, sibling).start()

    def words_of(which, sem):
        @pl.when(core == which)
        def _():
            wait_bytes(sw.at[pl.ds(0, 8)], sem)

        @pl.when(core != which)
        def _():
            wait_bytes(sw.at[pl.ds(8, 6)], sem)

    def unpack(b):
        words = jnp.concatenate([sw[b, q].astype(jnp.int32)[:, 0:208] for q in range(NDP)], axis=1)
        for k in range(16):
            st[16 * k:16 * k + 16, :] = jnp.where((words & (1 << k)) == 0, 1.0, -1.0).astype(BF)

    def z_first(c):
        return (lax.rem(c, 3) == 0) & (c < ZEND)

    def chain(c, step, first):
        sign = 1 - 2 * lax.rem(c, 2)
        buf, ss, rs, m = (zr2, zz_send, zz_recv, c // 3) if first else (zr, z_send, z_recv, c)
        for way, base, steps in ((1, 0, 4), (-1, 4, 3)):
            if step > steps:
                continue
            owner = lax.rem(z + way * sign * (steps + 1 - step) + 8, 8)
            term = own.at[c, owner] if first else own.at[c, owner, xh]
            if step > 1:
                src = buf.at[m, base + step - 2]
                wait_bytes(src, rs.at[m, base + step - 2])
                src[...] = (src[...].astype(F32) + term[...].astype(F32)).astype(BF)
            else:
                src = term
            to = lax.rem(z + way * sign + 8, 8) * 2 + xh
            remote(src, buf.at[m, base + step - 1], ss, rs.at[m, base + step - 1], to, t).start()

    def z_total(c, first):
        buf, rs, m = (zr2, zz_recv, c // 3) if first else (zr, z_recv, c)
        term = own[c, z] if first else own[c, z, xh]
        wait_bytes(buf.at[m, 3], rs.at[m, 3])
        wait_bytes(buf.at[m, 6], rs.at[m, 6])
        return term.astype(F32) + buf[m, 3].astype(F32) + buf[m, 6].astype(F32)

    def z_step(step):
        def stage(c):
            @pl.when(z_first(c))
            def _():
                if step < 4:
                    chain(c, step + 1, True)
                else:
                    own[c, z] = z_total(c, True).astype(BF)
                    remote(own.at[c, z, 1 - xh], xr2.at[c // 3], x2_send, x2_recv.at[c // 3], partner, t).start()

            @pl.when(jnp.logical_not(z_first(c)))
            def _():
                if step == 1:
                    add_partner(c)
                chain(c, step, False)
        return stage

    def add_partner(c):
        wait_bytes(xr.at[c], x_recv.at[c])
        own[c, :, xh] = (own[c, :, xh].astype(F32) + xr[c].astype(F32)).astype(BF)

    def z_direct(c):
        add_partner(c)

        def send(j, carry):
            zz = lax.rem(z + j, 8)
            remote(own.at[c, zz, xh], zr.at[c, j - 1], z_send, z_recv.at[c, 0], zz * 2 + xh, t).start()
            return carry

        lax.fori_loop(1, 8, send, 0)

    def activate(c, total):
        gate, up = total[:, 0:256], total[:, 256:512]
        hs[c] = (gate / (1.0 + jnp.exp(-gate)) * up).astype(BF)

    def hidden_chain(c):
        @pl.when(z_first(c))
        def _():
            wait_bytes(xr2.at[c // 3], x2_recv.at[c // 3])
            activate(c, own[c, z, xh].astype(F32) + xr2[c // 3].astype(F32))

        @pl.when(jnp.logical_not(z_first(c)))
        def _():
            activate(c, z_total(c, False))

        send_hidden(c)

    def hidden_direct(c):
        wait_bytes(zr.at[c], z_recv.at[c, 0])
        total = own[c, z, xh].astype(F32)
        for j in range(7):
            total = total + zr[c, j].astype(F32)
        activate(c, total)
        send_hidden(c)

    def send_hidden(c):
        @pl.when(t == c)
        def _():
            w1r[t] = hs[c]

        @pl.when(t != c)
        def _():
            remote(hs.at[c], w1r.at[t], w1_send, w1_recv, d, c).start()

    def mix(c):
        @pl.when(t == c)
        def _():
            wait_bytes(w1r.at[pl.ds(0, NT - 1)], w1_recv)
            turned = jnp.dot(w1r[...].reshape(256, 256), perm_h[...], preferred_element_type=F32).astype(BF)
            mixed = jnp.dot(walsh[...], turned, preferred_element_type=F32) * (1.0 / math.sqrt(FF))
            v[...] = mixed.astype(BF).reshape(16, 16, 256)
            g[c, z, xh] = v[t]

            def send(j, carry):
                to = lax.rem(t + j, NT)
                remote(v.at[to], g.at[c, z, xh], w2_send, w2_recv.at[c], d, to).start()
                return carry

            lax.fori_loop(1, NT, send, 0)

    def gather_z(b):
        @pl.when(t != b)
        def _():
            wait_bytes(g.at[b, z, xh], w2_recv.at[b])

        def send(j, carry):
            zz = lax.rem(z + j, 8)
            remote(g.at[b, z, xh], g.at[b, z, xh], g_send, g_recv.at[b], zz * 2 + xh, t).start()
            return carry

        lax.fori_loop(1, 8, send, 0)

    def gather_x(b):
        wait_bytes(g.at[b, pl.ds(0, 7), xh], g_recv.at[b])
        half = g.at[b, :, xh]
        remote(half, half, gx_send, gx_recv.at[b], partner, t).start()

    def turn(b):
        wait_bytes(g.at[b, :, 1 - xh], gx_recv.at[b])
        unpack(b)
        left = g[b].reshape(256, 256)
        for n in range(NB):
            cols = slice(256 * n, 256 * n + 256)
            racc[:, cols] += jnp.dot(left, st[:, cols], preferred_element_type=F32)

    def during(i, lag, stage, first, last):
        @pl.when((i >= first + lag) & (i < last + lag))
        def _():
            stage(i - lag)

    def each(i, lags, stage):
        if lags[0] == lags[1]:
            during(i, lags[0], stage, 0, NB)
        else:
            during(i, lags[0], stage, 0, NE)
            during(i, lags[1], stage, NE, NB)

    racc[...] = jnp.zeros_like(racc)

    def tick(i, carry):
        during(i, 0, gate_up, 0, NB)
        if NE:
            for step in range(1, 5):
                during(i, LAG_Z[0] + step - 1, z_step(step), 0, NE)
        during(i, LAG_Z[1], z_direct, NE, NB)
        if NE:
            during(i, LAG_H[0], hidden_chain, 0, NE)
        during(i, LAG_H[1], hidden_direct, NE, NB)
        each(i, LAG_W, mix)
        each(i, LAG_G, gather_z)
        each(i, LAG_X, gather_x)

        @pl.when(i == T_SHARE)
        def _():
            share_words()

        during(i, 1, down_weights, 0, NB)

        @pl.when(i == T_SIBLING)
        def _():
            words_to_sibling()

        @pl.when(i == T_WORDS)
        def _():
            words_of(1, s3_sem.at[1])

        each(i, LAG_S, turn)
        return carry

    lax.fori_loop(0, TICKS, tick, 0)

    rot[...] = racc[...].astype(BF).reshape(16, 16, HB)
    top = jnp.max(jnp.abs(rot[d].astype(F32)), axis=1, keepdims=True)
    pk[...] = jnp.broadcast_to(top, (16, 128))
    pr[t] = pk[...]

    def send_peak(j, carry):
        remote(pk, pr.at[t], p_send, p_recv, d, lax.rem(t + j, NT)).start()
        return carry

    lax.fori_loop(1, NT, send_peak, 0)

    width = 1024 // NOUT
    for n in range(NOUT):
        cols = slice(width * n, width * n + width)
        part = jnp.dot(rot[...].reshape(256, HB), dw[:, cols], preferred_element_type=F32)
        es[n] = part.astype(BF).reshape(16, 16, width)
        er[n, t] = es[n, t]

        def send_out(j, carry, n=n):
            to = lax.rem(t + j, NT)
            remote(es.at[n, to], er.at[n, t], e_send.at[n], e_recv.at[n], d, to).start()
            return carry

        lax.fori_loop(1, NT, send_out, 0)

    wait_bytes(pr.at[pl.ds(0, NT - 1)], p_recv)
    high = pr[0]
    for q in range(1, NT):
        high = jnp.maximum(high, pr[q])
    peak[...] = jnp.transpose(high)[0:1, :]

    for n in range(NOUT):
        wait_bytes(er.at[n, pl.ds(0, NT - 1)], e_recv.at[n])
        total = er[n, 0].astype(F32)
        for q in range(1, NT):
            total = total + er[n, q].astype(F32)
        total = total.astype(BF)
        for m in range(width // 256):
            lo = width * n + 256 * m
            out[:, lo:lo + 256] = jnp.dot(
                total[:, 256 * m:256 * m + 256], perm_out[...], preferred_element_type=F32).astype(BF)

    wait_bytes(x.at[core, pl.ds(0, NDP - 1)], a_send)
    sib.wait_send()

    @pl.when(s < 7)
    def _():
        wait_bytes(sw.at[pl.ds(0, 2), pl.ds(0, NDP - 1)], s1_send)
        wait_bytes(sw.at[pl.ds(0, 6)], s2_send)

    words_of(0, s3_sem.at[0])
    wait_bytes(xr.at[pl.ds(0, NB - NZF)], x_send)
    wait_bytes(zr.at[pl.ds(0, NB - NZF)], z_send)
    if NZF:
        wait_bytes(xr2, x2_send)
        wait_bytes(zr2, zz_send)

    @pl.when(t < NB)
    def _():
        wait_bytes(hs.at[pl.ds(0, NB - 1)], w1_send)
        wait_bytes(v.at[pl.ds(0, NT - 1)], w2_send)

    @pl.when(t >= NB)
    def _():
        wait_bytes(hs, w1_send)

    wait_bytes(g.at[:, pl.ds(0, 7), 0], g_send)
    wait_bytes(g.at[:, :, 0], gx_send)
    for n in range(NOUT):
        wait_bytes(es.at[n, pl.ds(0, NT - 1)], e_send.at[n])
    wait_bytes(pr.at[pl.ds(0, NT - 1)], p_send)


def local(tokens, gc, gs, uc, us, dc, ds, sb):
    dma = pltpu.SemaphoreType.DMA
    vm = pltpu.VMEM
    any_spec = pl.BlockSpec(memory_space=pl.ANY)
    vm_spec = pl.BlockSpec(memory_space=pltpu.VMEM)
    width = 1024 // NOUT
    out, peak = pl.pallas_call(
        body,
        out_shape=(jax.ShapeDtypeStruct((16, 1024), BF), jax.ShapeDtypeStruct((1, 16), F32)),
        in_specs=[any_spec, any_spec, vm_spec, any_spec, vm_spec, any_spec, vm_spec, vm_spec],
        out_specs=(vm_spec, vm_spec),
        scratch_shapes=[
            vm((2, 16, 16, 512), BF),
            vm((NB, 1024, 128), BF),
            vm((NB, 1024, 128), BF),
            vm((HB, 512), BF),
            vm((NB, 8, 2, 16, 512), BF),
            vm((NB, 8, 16, 512), BF),
            vm((NB, 7, 16, 512), BF),
            vm((max(NZF, 1), 7, 2, 16, 512), BF),
            vm((max(NZF, 1), 16, 512), BF),
            vm((NB, 16, 256), BF),
            vm((16, 16, 256), BF),
            vm((16, 16, 256), BF),
            vm((NB, 8, 2, 16, 256), BF),
            vm((14, 16, 16, 256), jnp.int16),
            vm((256, HB), BF),
            vm((HB, 1024), BF),
            vm((256, HB), F32),
            vm((16, 16, HB), BF),
            vm((NOUT, 16, 16, width), BF),
            vm((NOUT, 16, 16, width), BF),
            vm((16, 128), F32),
            vm((16, 16, 128), F32),
            vm((NB, 8, 256), F32),
            vm((NB, 8, 256), F32),
            vm((26, 1024), F32),
            vm((256, 256), jnp.int32),
            vm((16, 16, 256), jnp.int32),
            vm((1024, 512), BF),
            vm((256, 256), BF),
            vm((256, 256), BF),
            vm((256, 256), BF),
            vm((256, 256), BF),
            dma((2, NB)), dma, dma, dma, dma, dma((2,)), dma, dma, dma, dma((4,)),
            dma((2,)), dma, dma((NB,)), dma, dma((max(NZF, 1),)), dma, dma((NB, 7)), dma, dma((max(NZF, 1), 7)), dma, dma, dma, dma((NB,)), dma, dma((NB,)),
            dma, dma((NB,)), dma((NOUT,)), dma((NOUT,)), dma, dma,
        ],
        compiler_params=pltpu.CompilerParams(
            collective_id=0, has_side_effects=True, vmem_limit_bytes=63 * 1024 * 1024),
    )(tokens, gc, gs, uc, us, dc, ds, sb)

    def hand_on(a, b, c, e, sems):
        copies = (pltpu.make_async_copy(a, c, sems.at[0]), pltpu.make_async_copy(b, e, sems.at[1]))
        for copy in copies:
            copy.start()
        for copy in copies:
            copy.wait()

    out, peak = pl.pallas_call(
        hand_on, out_shape=(jax.ShapeDtypeStruct((16, 1024), BF), jax.ShapeDtypeStruct((1, 16), F32)),
        in_specs=[any_spec, any_spec], out_specs=(any_spec, any_spec), scratch_shapes=[dma((2,))],
        compiler_params=pltpu.CompilerParams(vmem_limit_bytes=63 * 1024 * 1024))(out, peak)
    return out, peak.reshape(16)


def solution(mesh):
    return jax.shard_map(
        local,
        mesh=mesh,
        in_specs=(
            P("dp", None),
            P("dp", "tensor"),
            P("dp", "tensor"),
            P("dp", "tensor"),
            P("dp", "tensor"),
            P("tensor", "dp"),
            P("tensor", "dp"),
            P("dp", None),
        ),
        out_specs=(P("tensor", "dp"), P("dp")),
        check_vma=False,
    )
```

```python
import math

import jax
import jax.numpy as jnp
from jax import lax
from jax.experimental import pallas as pl
from jax.experimental.pallas import tpu as pltpu
from jax.sharding import PartitionSpec as P

FF = 53248
HB = 3328
NB = 13
NDP = 16
NT = 16
MESH = pl.DeviceIdType.MESH
BF = jnp.bfloat16
F32 = jnp.float32

NE = 9
ZEND = 8
NZF = ZEND // 2
NG = 1
ORDER = (131328, 318723, 2164229, 1050631, 657699, 1182501, 13644071, 3350540, 3478737, 3613394, 4265683, 4445232, 4528164, 4707634, 4215078, 14051806, 14103635, 4347176, 5757034, 7395638, 4512363, 7527224, 7986284, 7697265, 4618112, 9011834, 4751732, 8881539, 9075600, 7901814, 10058884, 9802641, 8817559, 8952480, 10654860, 9873819, 11591585, 10734744, 10990245, 11643577, 11252644, 12035765, 11844264, 11975867, 16777144)

NOUT = 2


def eo_column(p):
    return jnp.where(p < 128, 2 * p, 2 * (p - 128) + 1)


def one_hot(cond):
    return jnp.where(cond, 1.0, 0.0).astype(BF)


def body(tokens, gc, gs, uc, us, dc, ds, sb, out, peak,
         x, gcv, ucv, dcv, own, xr, zr, zr2, xr2, hs, w1r, v, g, sw, st, dw, racc, rot, es, er, pk, pr,
         gsv, usv, dsv, sbp, sbt, wb, perm_in, perm_h, perm_out, walsh,
         code_sem, dcode_sem, loc_sem, a_send, a_recv, sib_sem, s1_send, s1_recv, s2_send, s2_recv,
         s3_sem, x_send, x_recv, x2_send, x2_recv, z_send, z_recv, zz_send, zz_recv, gl_send, w1_send, w1_recv, w2_send, w2_recv, g_send, g_recv,
         gx_send, gx_recv, e_send, e_recv, p_send, p_recv):
    d = lax.axis_index("dp")
    t = lax.axis_index("tensor")
    core = lax.rem(t, 2)
    y = lax.rem(t // 2, 4)
    s = core * 4 + y
    z = d // 2
    xh = lax.rem(d, 2)
    partner = z * 2 + (1 - xh)
    sibling = t + 1 - 2 * core

    def remote(src, dst, ssem, rsem, dp, tn):
        return pltpu.make_async_remote_copy(
            src_ref=src, dst_ref=dst, send_sem=ssem, recv_sem=rsem, device_id=(dp, tn), device_id_type=MESH)

    def wait_bytes(ref, sem):
        pltpu.make_async_copy(ref, ref, sem).wait()

    barrier = pltpu.get_barrier_semaphore()

    def greet(j, carry):
        pl.semaphore_signal(barrier, inc=1, device_id=(lax.rem(d + j, NDP), t), device_id_type=MESH)
        pl.semaphore_signal(barrier, inc=1, device_id=(d, lax.rem(t + j, NT)), device_id_type=MESH)
        return carry

    lax.fori_loop(1, NDP, greet, 0)

    def code_copies(c):
        lanes = pl.ds(pl.multiple_of(c * 128, 128), 128)
        return (pltpu.make_async_copy(gc.at[:, lanes], gcv.at[c], code_sem.at[0, c]),
                pltpu.make_async_copy(uc.at[:, lanes], ucv.at[c], code_sem.at[1, c]))

    def start_codes(c, carry):
        for copy in code_copies(c):
            copy.start()
        return carry

    lax.fori_loop(0, NB, start_codes, 0)
    dcopy = pltpu.make_async_copy(dc, dcv, dcode_sem)
    dcopy.start()

    sbp[...] = jnp.zeros_like(sbp)
    sbp[0:208, 0:208] = sb[...]
    sbt[...] = jnp.transpose(sbp[...]).reshape(16, 16, 256)

    @pl.when(s < 7)
    def _():
        for u in range(2):
            sw[2 * s + u, d] = sbt[2 * s + u].astype(jnp.int16)

    pl.semaphore_wait(barrier, 2 * (NDP - 1))

    def token_copy(dst_dp):
        lanes = pl.ds(pl.multiple_of(dst_dp * 1024 + core * 512, 512), 512)
        return tokens.at[:, lanes]

    def send_tokens(j, carry):
        to = lax.rem(d + j, NDP)
        remote(token_copy(to), x.at[core, d], a_send, a_recv, to, t).start()
        return carry

    lax.fori_loop(1, NDP, send_tokens, 0)
    mine = pltpu.make_async_copy(token_copy(d), x.at[core, d], loc_sem)
    mine.start()

    @pl.when(s < 7)
    def _():
        def send_words(j, carry):
            part = sw.at[pl.ds(2 * s, 2), d]
            remote(part, part, s1_send, s1_recv, lax.rem(d + j, NDP), t).start()
            return carry

        lax.fori_loop(1, NDP, send_words, 0)

    src = lax.broadcasted_iota(jnp.int32, (256, 256), 0)
    dst = lax.broadcasted_iota(jnp.int32, (256, 256), 1)
    perm_in[...] = one_hot(src == eo_column(dst))
    perm_out[...] = one_hot(dst == eo_column(src))
    perm_h[...] = one_hot(eo_column(src) == 16 * (dst & 15) + (dst >> 4))
    both = (src >> 4) & (dst >> 4)
    odd = (both ^ (both >> 1) ^ (both >> 2) ^ (both >> 3)) & 1
    walsh[...] = jnp.where((src & 15) == (dst & 15), jnp.where(odd == 1, -1.0, 1.0), 0.0).astype(BF)

    for b in range(NB):
        cols = slice(256 * b, 256 * b + 256)
        gsv[b] = jnp.dot(gs[:, cols], perm_in[...], preferred_element_type=F32)
        usv[b] = jnp.dot(us[:, cols], perm_in[...], preferred_element_type=F32)
    for n in range(4):
        cols = slice(256 * n, 256 * n + 256)
        dsv[:, cols] = jnp.dot(ds[:, cols], perm_in[...], preferred_element_type=F32)

    wait_bytes(x.at[core, pl.ds(0, NDP - 1)], a_recv)
    mine.wait()
    sib = remote(x.at[core], x.at[core], sib_sem.at[0], sib_sem.at[1], d, sibling)
    sib.start()
    sib.wait_recv()

    def nibbles(codes):
        whole = codes.astype(F32)
        high = jnp.floor(whole * 0.0625)
        return whole - 16.0 * high - 8.0, high - 8.0

    def gate_up(c):
        for copy in code_copies(c):
            copy.wait()
        for base, codes, scales in ((0, gcv, gsv), (256, ucv, usv)):
            for r in range(8):
                rows = slice(128 * r, 128 * r + 128)
                low, high = nibbles(codes[c, rows, :])
                sc = scales[c, r:r + 1, :]
                wb[rows, base:base + 128] = (low * sc[:, 0:128]).astype(BF)
                wb[rows, base + 128:base + 256] = (high * sc[:, 128:256]).astype(BF)
        part = jnp.dot(x[0].reshape(256, 512), wb[0:512, :], preferred_element_type=F32)
        part = part + jnp.dot(x[1].reshape(256, 512), wb[512:1024, :], preferred_element_type=F32)
        own[c] = part.astype(BF).reshape(8, 2, 16, 512)

        @pl.when(z_first(c))
        def _():
            chain(c, 1, True)

        @pl.when(jnp.logical_not(z_first(c)))
        def _():
            remote(own.at[c, :, 1 - xh], xr.at[c], x_send, x_recv.at[c], partner, t).start()

    def down_weights(b):
        @pl.when(b == 0)
        def _():
            dcopy.wait()

        for r in range(2):
            rows = pl.ds(pl.multiple_of(256 * b + 128 * r, 128), 128)
            low, high = nibbles(dcv[rows, :])
            sc = dsv[pl.ds(2 * b + r, 1), :]
            for n in range(4):
                words = slice(128 * n, 128 * n + 128)
                dw[rows, 256 * n:256 * n + 128] = (low[:, words] * sc[:, 256 * n:256 * n + 128]).astype(BF)
                dw[rows, 256 * n + 128:256 * n + 256] = (high[:, words] * sc[:, 256 * n + 128:256 * n + 256]).astype(BF)

    def share_words():
        @pl.when(s < 7)
        def _():
            wait_bytes(sw.at[pl.ds(0, 2), pl.ds(0, NDP - 1)], s1_recv)

            def send(j, carry):
                to = t + 2 * (lax.rem(y + j, 4) - y)
                part = sw.at[pl.ds(2 * s, 2)]
                remote(part, part, s2_send, s2_recv.at[y], d, to).start()
                return carry

            lax.fori_loop(1, 4, send, 0)

    def words_to_sibling():
        for q in range(4):
            @pl.when((y != q) & (core * 4 + q < 7))
            def _():
                wait_bytes(sw.at[pl.ds(2 * q, 2)], s2_recv.at[q])

        @pl.when(core == 0)
        def _():
            remote(sw.at[pl.ds(0, 8)], sw.at[pl.ds(0, 8)], s3_sem.at[0], s3_sem.at[1], d, sibling).start()

        @pl.when(core == 1)
        def _():
            remote(sw.at[pl.ds(8, 6)], sw.at[pl.ds(8, 6)], s3_sem.at[0], s3_sem.at[1], d, sibling).start()

    def words_of(which, sem):
        @pl.when(core == which)
        def _():
            wait_bytes(sw.at[pl.ds(0, 8)], sem)

        @pl.when(core != which)
        def _():
            wait_bytes(sw.at[pl.ds(8, 6)], sem)

    def unpack(b):
        words = jnp.concatenate([sw[b, q].astype(jnp.int32)[:, 0:208] for q in range(NDP)], axis=1)
        for k in range(16):
            st[16 * k:16 * k + 16, :] = jnp.where((words & (1 << k)) == 0, 1.0, -1.0).astype(BF)

    def z_first(c):
        return (lax.rem(c, 2) == 1) & (c < ZEND)

    def chain(c, step, first):
        sign = 1 - 2 * lax.rem(c, 2)
        buf, ss, rs, m = (zr2, zz_send, zz_recv, c // 2) if first else (zr, z_send, z_recv, c)
        for way, base, steps in ((1, 0, 4), (-1, 4, 3)):
            if step > steps:
                continue
            owner = lax.rem(z + way * sign * (steps + 1 - step) + 8, 8)
            term = own.at[c, owner] if first else own.at[c, owner, xh]
            if step > 1:
                src = buf.at[m, base + step - 2]
                wait_bytes(src, rs.at[m, base + step - 2])
                src[...] = (src[...].astype(F32) + term[...].astype(F32)).astype(BF)
            else:
                src = term
            to = lax.rem(z + way * sign + 8, 8) * 2 + xh
            remote(src, buf.at[m, base + step - 1], ss, rs.at[m, base + step - 1], to, t).start()

    def z_total(c, first):
        buf, rs, m = (zr2, zz_recv, c // 2) if first else (zr, z_recv, c)
        term = own[c, z] if first else own[c, z, xh]
        wait_bytes(buf.at[m, 3], rs.at[m, 3])
        wait_bytes(buf.at[m, 6], rs.at[m, 6])
        return term.astype(F32) + buf[m, 3].astype(F32) + buf[m, 6].astype(F32)

    def chain_start(c):
        add_partner(c)
        chain(c, 1, False)

    def chain_on(step):
        def stage(c):
            @pl.when(z_first(c))
            def _():
                chain(c, step, True)

            @pl.when(jnp.logical_not(z_first(c)))
            def _():
                chain(c, step, False)
        return stage

    def chain_end(c):
        own[c, z] = z_total(c, True).astype(BF)
        remote(own.at[c, z, 1 - xh], xr2.at[c // 2], x2_send, x2_recv.at[c // 2], partner, t).start()

    def add_partner(c):
        wait_bytes(xr.at[c], x_recv.at[c])
        own[c, :, xh] = (own[c, :, xh].astype(F32) + xr[c].astype(F32)).astype(BF)

    def z_direct(c):
        add_partner(c)

        def send(j, carry):
            zz = lax.rem(z + j, 8)
            remote(own.at[c, zz, xh], zr.at[c, j - 1], z_send, z_recv.at[c, 0], zz * 2 + xh, t).start()
            return carry

        lax.fori_loop(1, 8, send, 0)

    def activate(c, total):
        gate, up = total[:, 0:256], total[:, 256:512]
        hs[c] = (gate / (1.0 + jnp.exp(-gate)) * up).astype(BF)

    def hidden(c):
        @pl.when(z_first(c))
        def _():
            wait_bytes(xr2.at[c // 2], x2_recv.at[c // 2])
            activate(c, own[c, z, xh].astype(F32) + xr2[c // 2].astype(F32))

        @pl.when((c < NE) & jnp.logical_not(z_first(c)))
        def _():
            activate(c, z_total(c, False))

        @pl.when(c >= NE)
        def _():
            wait_bytes(zr.at[c], z_recv.at[c, 0])
            total = own[c, z, xh].astype(F32)
            for j in range(7):
                total = total + zr[c, j].astype(F32)
            activate(c, total)

        send_hidden(c)

    def send_hidden(c):
        @pl.when(t == c)
        def _():
            w1r[t] = hs[c]

        @pl.when(t != c)
        def _():
            remote(hs.at[c], w1r.at[t], w1_send, w1_recv, d, c).start()

    def mix(c):
        @pl.when(t == c)
        def _():
            wait_bytes(w1r.at[pl.ds(0, NT - 1)], w1_recv)
            turned = jnp.dot(w1r[...].reshape(256, 256), perm_h[...], preferred_element_type=F32).astype(BF)
            mixed = jnp.dot(walsh[...], turned, preferred_element_type=F32) * (1.0 / math.sqrt(FF))
            v[...] = mixed.astype(BF).reshape(16, 16, 256)
            g[c, z, xh] = v[t]

            def send(j, carry):
                to = lax.rem(t + j, NT)
                remote(v.at[to], g.at[c, z, xh], w2_send, w2_recv.at[c], d, to).start()
                return carry

            lax.fori_loop(1, NT, send, 0)

    def wait_mixed(b):
        @pl.when(t != b)
        def _():
            wait_bytes(g.at[b, z, xh], w2_recv.at[b])

    def gather_all(b):
        wait_mixed(b)

        def send(j, carry):
            part = g.at[b, z, xh]
            remote(part, part, gl_send, g_recv.at[b], lax.rem(d + j, NDP), t).start()
            return carry

        lax.fori_loop(1, NDP, send, 0)

    def gather_z(b):
        wait_mixed(b)

        def send(j, carry):
            zz = lax.rem(z + j, 8)
            remote(g.at[b, z, xh], g.at[b, z, xh], g_send, g_recv.at[b], zz * 2 + xh, t).start()
            return carry

        lax.fori_loop(1, 8, send, 0)

    def gather_x(b):
        wait_bytes(g.at[b, pl.ds(0, 7), xh], g_recv.at[b])
        half = g.at[b, :, xh]
        remote(half, half, gx_send, gx_recv.at[b], partner, t).start()

    def turn(b):
        @pl.when(b < NB - NG)
        def _():
            wait_bytes(g.at[b, :, 1 - xh], gx_recv.at[b])

        @pl.when(b >= NB - NG)
        def _():
            wait_bytes(v.at[pl.ds(0, NDP - 1)], g_recv.at[b])

        unpack(b)
        left = g[b].reshape(256, 256)
        for n in range(NB):
            cols = slice(256 * n, 256 * n + 256)
            racc[:, cols] += jnp.dot(left, st[:, cols], preferred_element_type=F32)

    def aside(b):
        @pl.when(b < NB)
        def _():
            down_weights(b)

        @pl.when(b == 13)
        def _():
            share_words()

        @pl.when(b == 14)
        def _():
            words_to_sibling()

        @pl.when(b == 15)
        def _():
            words_of(1, s3_sem.at[1])

    stages = (gate_up, chain_start, chain_on(2), chain_on(3), chain_on(4), chain_end, z_direct, hidden, mix, gather_z,
              gather_x, turn, gather_all, aside)
    racc[...] = jnp.zeros_like(racc)

    def three(i, carry):
        codes = jnp.int32(0)
        for k, number in enumerate(ORDER):
            codes = jnp.where(i == k, number, codes)

        def one(j, codes):
            code = lax.rem(codes, 256)
            block = lax.rem(code, 16)
            for k, stage in enumerate(stages):
                @pl.when(code // 16 == k)
                def _():
                    stage(block)
            return codes // 256

        lax.fori_loop(0, 3, one, codes)
        return carry

    lax.fori_loop(0, len(ORDER), three, 0)

    rot[...] = racc[...].astype(BF).reshape(16, 16, HB)
    top = jnp.max(jnp.abs(rot[d].astype(F32)), axis=1, keepdims=True)
    pk[...] = jnp.broadcast_to(top, (16, 128))
    pr[t] = pk[...]

    def send_peak(j, carry):
        remote(pk, pr.at[t], p_send, p_recv, d, lax.rem(t + j, NT)).start()
        return carry

    lax.fori_loop(1, NT, send_peak, 0)

    width = 1024 // NOUT
    for n in range(NOUT):
        cols = slice(width * n, width * n + width)
        part = jnp.dot(rot[...].reshape(256, HB), dw[:, cols], preferred_element_type=F32)
        es[n] = part.astype(BF).reshape(16, 16, width)
        er[n, t] = es[n, t]

        def send_out(j, carry, n=n):
            to = lax.rem(t + j, NT)
            remote(es.at[n, to], er.at[n, t], e_send.at[n], e_recv.at[n], d, to).start()
            return carry

        lax.fori_loop(1, NT, send_out, 0)

    wait_bytes(pr.at[pl.ds(0, NT - 1)], p_recv)
    high = pr[0]
    for q in range(1, NT):
        high = jnp.maximum(high, pr[q])
    peak[...] = jnp.transpose(high)[0:1, :]

    for n in range(NOUT):
        wait_bytes(er.at[n, pl.ds(0, NT - 1)], e_recv.at[n])
        total = er[n, 0].astype(F32)
        for q in range(1, NT):
            total = total + er[n, q].astype(F32)
        total = total.astype(BF)
        for m in range(width // 256):
            lo = width * n + 256 * m
            out[:, lo:lo + 256] = jnp.dot(
                total[:, 256 * m:256 * m + 256], perm_out[...], preferred_element_type=F32).astype(BF)

    wait_bytes(x.at[core, pl.ds(0, NDP - 1)], a_send)
    sib.wait_send()

    @pl.when(s < 7)
    def _():
        wait_bytes(sw.at[pl.ds(0, 2), pl.ds(0, NDP - 1)], s1_send)
        wait_bytes(sw.at[pl.ds(0, 6)], s2_send)

    words_of(0, s3_sem.at[0])
    wait_bytes(xr.at[pl.ds(0, NB - NZF)], x_send)
    wait_bytes(zr.at[pl.ds(0, NB - NZF)], z_send)
    if NG:
        wait_bytes(v.at[pl.ds(0, NDP - 1)], gl_send)
    if NZF:
        wait_bytes(xr2, x2_send)
        wait_bytes(zr2, zz_send)

    @pl.when(t < NB)
    def _():
        wait_bytes(hs.at[pl.ds(0, NB - 1)], w1_send)
        wait_bytes(v.at[pl.ds(0, NT - 1)], w2_send)

    @pl.when(t >= NB)
    def _():
        wait_bytes(hs, w1_send)

    wait_bytes(g.at[pl.ds(0, NB - NG), pl.ds(0, 7), 0], g_send)
    wait_bytes(g.at[pl.ds(0, NB - NG), :, 0], gx_send)
    for n in range(NOUT):
        wait_bytes(es.at[n, pl.ds(0, NT - 1)], e_send.at[n])
    wait_bytes(pr.at[pl.ds(0, NT - 1)], p_send)


def local(tokens, gc, gs, uc, us, dc, ds, sb):
    dma = pltpu.SemaphoreType.DMA
    vm = pltpu.VMEM
    any_spec = pl.BlockSpec(memory_space=pl.ANY)
    vm_spec = pl.BlockSpec(memory_space=pltpu.VMEM)
    width = 1024 // NOUT
    out, peak = pl.pallas_call(
        body,
        out_shape=(jax.ShapeDtypeStruct((16, 1024), BF), jax.ShapeDtypeStruct((1, 16), F32)),
        in_specs=[any_spec, any_spec, vm_spec, any_spec, vm_spec, any_spec, vm_spec, vm_spec],
        out_specs=(vm_spec, vm_spec),
        scratch_shapes=[
            vm((2, 16, 16, 512), BF),
            vm((NB, 1024, 128), BF),
            vm((NB, 1024, 128), BF),
            vm((HB, 512), BF),
            vm((NB, 8, 2, 16, 512), BF),
            vm((NB, 8, 16, 512), BF),
            vm((NB, 7, 16, 512), BF),
            vm((max(NZF, 1), 7, 2, 16, 512), BF),
            vm((max(NZF, 1), 16, 512), BF),
            vm((NB, 16, 256), BF),
            vm((16, 16, 256), BF),
            vm((16, 16, 256), BF),
            vm((NB, 8, 2, 16, 256), BF),
            vm((14, 16, 16, 256), jnp.int16),
            vm((256, HB), BF),
            vm((HB, 1024), BF),
            vm((256, HB), F32),
            vm((16, 16, HB), BF),
            vm((NOUT, 16, 16, width), BF),
            vm((NOUT, 16, 16, width), BF),
            vm((16, 128), F32),
            vm((16, 16, 128), F32),
            vm((NB, 8, 256), F32),
            vm((NB, 8, 256), F32),
            vm((26, 1024), F32),
            vm((256, 256), jnp.int32),
            vm((16, 16, 256), jnp.int32),
            vm((1024, 512), BF),
            vm((256, 256), BF),
            vm((256, 256), BF),
            vm((256, 256), BF),
            vm((256, 256), BF),
            dma((2, NB)), dma, dma, dma, dma, dma((2,)), dma, dma, dma, dma((4,)),
            dma((2,)), dma, dma((NB,)), dma, dma((max(NZF, 1),)), dma, dma((NB, 7)), dma, dma((max(NZF, 1), 7)), dma, dma, dma, dma, dma((NB,)), dma, dma((NB,)),
            dma, dma((NB,)), dma((NOUT,)), dma((NOUT,)), dma, dma,
        ],
        compiler_params=pltpu.CompilerParams(
            collective_id=0, has_side_effects=True, vmem_limit_bytes=63 * 1024 * 1024),
    )(tokens, gc, gs, uc, us, dc, ds, sb)

    def hand_on(a, b, c, e, sems):
        copies = (pltpu.make_async_copy(a, c, sems.at[0]), pltpu.make_async_copy(b, e, sems.at[1]))
        for copy in copies:
            copy.start()
        for copy in copies:
            copy.wait()

    out, peak = pl.pallas_call(
        hand_on, out_shape=(jax.ShapeDtypeStruct((16, 1024), BF), jax.ShapeDtypeStruct((1, 16), F32)),
        in_specs=[any_spec, any_spec], out_specs=(any_spec, any_spec), scratch_shapes=[dma((2,))],
        compiler_params=pltpu.CompilerParams(vmem_limit_bytes=63 * 1024 * 1024))(out, peak)
    return out, peak.reshape(16)


def solution(mesh):
    return jax.shard_map(
        local,
        mesh=mesh,
        in_specs=(
            P("dp", None),
            P("dp", "tensor"),
            P("dp", "tensor"),
            P("dp", "tensor"),
            P("dp", "tensor"),
            P("tensor", "dp"),
            P("tensor", "dp"),
            P("dp", None),
        ),
        out_specs=(P("tensor", "dp"), P("dp")),
        check_vma=False,
    )
```

```python
import functools
import math

import jax
import jax.numpy as jnp
from jax import lax
from jax.experimental import pallas as pl
from jax.experimental.pallas import tpu as pltpu
from jax.sharding import PartitionSpec as P

FF = 53248
HB = 3328
NB = 13
NDP = 16
NT = 16
MESH = pl.DeviceIdType.MESH
BF = jnp.bfloat16
F32 = jnp.float32

ZFIRST = (0, 1, 3, 4, 6, 8, 11)
DIRECT = ()
WIDE = (10, 12)
NZF = len(ZFIRST)
ORDER = (131328, 318723, 401413, 2295585, 599048, 1232944, 3221002, 3345361, 2627026, 13841420, 1516096, 4314166, 2442027, 13973529, 3297348, 1714134, 3887430, 5496535, 2742325, 7358492, 3621460, 5647065, 4541297, 14301555, 7493676, 7620480, 7789370, 5993857, 3965769, 7895004, 8669826, 8812944, 5012357, 8033169, 9603207, 9010324, 9803403, 9931424, 9214113, 10197411, 11591586, 11651748, 11783334, 10990245, 11118772, 11905974, 12236983, 12368825)

NOUT = 2


def among(c, blocks):
    return functools.reduce(jnp.logical_or, [c == k for k in blocks], c < 0)


def eo_column(p):
    return jnp.where(p < 128, 2 * p, 2 * (p - 128) + 1)


def one_hot(cond):
    return jnp.where(cond, 1.0, 0.0).astype(BF)


def body(tokens, gc, gs, uc, us, dc, ds, sb, out, peak,
         x, gcv, ucv, dcv, own, xr, zr, zr2, xr2, hs, w1r, v, g, sw, st, dw, racc, rot, es, er, pk, pr,
         gsv, usv, dsv, sbp, sbt, wb, perm_in, perm_h, perm_out, walsh,
         code_sem, dcode_sem, loc_sem, a_send, a_recv, sib_sem, s1_send, s1_recv, s2_send, s2_recv,
         s3_sem, x_send, x_recv, x2_send, x2_recv, z_send, z_recv, zz_send, zz_recv, gl_send, w1_send, w1_recv, w2_send, w2_recv, g_send, g_recv,
         gx_send, gx_recv, e_send, e_recv, p_send, p_recv):
    d = lax.axis_index("dp")
    t = lax.axis_index("tensor")
    core = lax.rem(t, 2)
    y = lax.rem(t // 2, 4)
    s = core * 4 + y
    z = d // 2
    xh = lax.rem(d, 2)
    partner = z * 2 + (1 - xh)
    sibling = t + 1 - 2 * core

    def remote(src, dst, ssem, rsem, dp, tn):
        return pltpu.make_async_remote_copy(
            src_ref=src, dst_ref=dst, send_sem=ssem, recv_sem=rsem, device_id=(dp, tn), device_id_type=MESH)

    def wait_bytes(ref, sem):
        pltpu.make_async_copy(ref, ref, sem).wait()

    barrier = pltpu.get_barrier_semaphore()

    def greet(j, carry):
        pl.semaphore_signal(barrier, inc=1, device_id=(lax.rem(d + j, NDP), t), device_id_type=MESH)
        pl.semaphore_signal(barrier, inc=1, device_id=(d, lax.rem(t + j, NT)), device_id_type=MESH)
        return carry

    lax.fori_loop(1, NDP, greet, 0)

    def code_copies(c):
        lanes = pl.ds(pl.multiple_of(c * 128, 128), 128)
        return (pltpu.make_async_copy(gc.at[:, lanes], gcv.at[c], code_sem.at[0, c]),
                pltpu.make_async_copy(uc.at[:, lanes], ucv.at[c], code_sem.at[1, c]))

    def start_codes(c, carry):
        for copy in code_copies(c):
            copy.start()
        return carry

    lax.fori_loop(0, NB, start_codes, 0)
    dcopy = pltpu.make_async_copy(dc, dcv, dcode_sem)
    dcopy.start()

    sbp[...] = jnp.zeros_like(sbp)
    sbp[0:208, 0:208] = sb[...]
    sbt[...] = jnp.transpose(sbp[...]).reshape(16, 16, 256)

    @pl.when(s < 7)
    def _():
        for u in range(2):
            sw[2 * s + u, d] = sbt[2 * s + u].astype(jnp.int16)

    pl.semaphore_wait(barrier, 2 * (NDP - 1))

    def token_copy(dst_dp):
        lanes = pl.ds(pl.multiple_of(dst_dp * 1024 + core * 512, 512), 512)
        return tokens.at[:, lanes]

    def send_tokens(j, carry):
        to = lax.rem(d + j, NDP)
        remote(token_copy(to), x.at[core, d], a_send, a_recv, to, t).start()
        return carry

    lax.fori_loop(1, NDP, send_tokens, 0)
    mine = pltpu.make_async_copy(token_copy(d), x.at[core, d], loc_sem)
    mine.start()

    @pl.when(s < 7)
    def _():
        def send_words(j, carry):
            part = sw.at[pl.ds(2 * s, 2), d]
            remote(part, part, s1_send, s1_recv, lax.rem(d + j, NDP), t).start()
            return carry

        lax.fori_loop(1, NDP, send_words, 0)

    src = lax.broadcasted_iota(jnp.int32, (256, 256), 0)
    dst = lax.broadcasted_iota(jnp.int32, (256, 256), 1)
    perm_in[...] = one_hot(src == eo_column(dst))
    perm_out[...] = one_hot(dst == eo_column(src))
    perm_h[...] = one_hot(eo_column(src) == 16 * (dst & 15) + (dst >> 4))
    both = (src >> 4) & (dst >> 4)
    odd = (both ^ (both >> 1) ^ (both >> 2) ^ (both >> 3)) & 1
    walsh[...] = jnp.where((src & 15) == (dst & 15), jnp.where(odd == 1, -1.0, 1.0), 0.0).astype(BF)

    racc[...] = jnp.zeros_like(racc)

    for b in range(NB):
        cols = slice(256 * b, 256 * b + 256)
        gsv[b] = jnp.dot(gs[:, cols], perm_in[...], preferred_element_type=F32)
        usv[b] = jnp.dot(us[:, cols], perm_in[...], preferred_element_type=F32)
    for n in range(4):
        cols = slice(256 * n, 256 * n + 256)
        dsv[:, cols] = jnp.dot(ds[:, cols], perm_in[...], preferred_element_type=F32)

    wait_bytes(x.at[core, pl.ds(0, NDP - 1)], a_recv)
    mine.wait()
    sib = remote(x.at[core], x.at[core], sib_sem.at[0], sib_sem.at[1], d, sibling)
    sib.start()
    sib.wait_recv()

    def nibbles(codes):
        whole = codes.astype(F32)
        high = jnp.floor(whole * 0.0625)
        return whole - 16.0 * high - 8.0, high - 8.0

    def gate_up(c):
        for copy in code_copies(c):
            copy.wait()
        for base, codes, scales in ((0, gcv, gsv), (256, ucv, usv)):
            for r in range(8):
                rows = slice(128 * r, 128 * r + 128)
                low, high = nibbles(codes[c, rows, :])
                sc = scales[c, r:r + 1, :]
                wb[rows, base:base + 128] = (low * sc[:, 0:128]).astype(BF)
                wb[rows, base + 128:base + 256] = (high * sc[:, 128:256]).astype(BF)
        part = jnp.dot(x[0].reshape(256, 512), wb[0:512, :], preferred_element_type=F32)
        part = part + jnp.dot(x[1].reshape(256, 512), wb[512:1024, :], preferred_element_type=F32)
        own[c] = part.astype(BF).reshape(8, 2, 16, 512)

        @pl.when(z_first(c))
        def _():
            chain(c, 1, True)

        @pl.when(jnp.logical_not(z_first(c)))
        def _():
            remote(own.at[c, :, 1 - xh], xr.at[c], x_send, x_recv.at[c], partner, t).start()

    def down_weights(b):
        @pl.when(b == 0)
        def _():
            dcopy.wait()

        for r in range(2):
            rows = pl.ds(pl.multiple_of(256 * b + 128 * r, 128), 128)
            low, high = nibbles(dcv[rows, :])
            sc = dsv[pl.ds(2 * b + r, 1), :]
            for n in range(4):
                words = slice(128 * n, 128 * n + 128)
                dw[rows, 256 * n:256 * n + 128] = (low[:, words] * sc[:, 256 * n:256 * n + 128]).astype(BF)
                dw[rows, 256 * n + 128:256 * n + 256] = (high[:, words] * sc[:, 256 * n + 128:256 * n + 256]).astype(BF)

    def share_words():
        @pl.when(s < 7)
        def _():
            wait_bytes(sw.at[pl.ds(0, 2), pl.ds(0, NDP - 1)], s1_recv)

            def send(j, carry):
                to = t + 2 * (lax.rem(y + j, 4) - y)
                part = sw.at[pl.ds(2 * s, 2)]
                remote(part, part, s2_send, s2_recv.at[y], d, to).start()
                return carry

            lax.fori_loop(1, 4, send, 0)

    def words_to_sibling():
        for q in range(4):
            @pl.when((y != q) & (core * 4 + q < 7))
            def _():
                wait_bytes(sw.at[pl.ds(2 * q, 2)], s2_recv.at[q])

        @pl.when(core == 0)
        def _():
            remote(sw.at[pl.ds(0, 8)], sw.at[pl.ds(0, 8)], s3_sem.at[0], s3_sem.at[1], d, sibling).start()

        @pl.when(core == 1)
        def _():
            remote(sw.at[pl.ds(8, 6)], sw.at[pl.ds(8, 6)], s3_sem.at[0], s3_sem.at[1], d, sibling).start()

    def words_of(which, sem):
        @pl.when(core == which)
        def _():
            wait_bytes(sw.at[pl.ds(0, 8)], sem)

        @pl.when(core != which)
        def _():
            wait_bytes(sw.at[pl.ds(8, 6)], sem)

    def unpack(b):
        words = jnp.concatenate([sw[b, q].astype(jnp.int32)[:, 0:208] for q in range(NDP)], axis=1)
        for k in range(16):
            st[16 * k:16 * k + 16, :] = jnp.where((words & (1 << k)) == 0, 1.0, -1.0).astype(BF)

    def z_first(c):
        return among(c, ZFIRST)

    def chain(c, step, first):
        sign = 1 - 2 * lax.rem(c, 2)
        buf, ss, rs, m = (zr2, zz_send, zz_recv, c) if first else (zr, z_send, z_recv, c)
        for way, base, steps in ((1, 0, 4), (-1, 4, 3)):
            if step > steps:
                continue
            owner = lax.rem(z + way * sign * (steps + 1 - step) + 8, 8)
            term = own.at[c, owner] if first else own.at[c, owner, xh]
            if step > 1:
                src = buf.at[m, base + step - 2]
                wait_bytes(src, rs.at[m, base + step - 2])
                src[...] = (src[...].astype(F32) + term[...].astype(F32)).astype(BF)
            else:
                src = term
            to = lax.rem(z + way * sign + 8, 8) * 2 + xh
            remote(src, buf.at[m, base + step - 1], ss, rs.at[m, base + step - 1], to, t).start()

    def z_total(c, first):
        buf, rs, m = (zr2, zz_recv, c) if first else (zr, z_recv, c)
        term = own[c, z] if first else own[c, z, xh]
        wait_bytes(buf.at[m, 3], rs.at[m, 3])
        wait_bytes(buf.at[m, 6], rs.at[m, 6])
        return term.astype(F32) + buf[m, 3].astype(F32) + buf[m, 6].astype(F32)

    def chain_start(c):
        add_partner(c)
        chain(c, 1, False)

    def chain_on(step):
        def stage(c):
            @pl.when(z_first(c))
            def _():
                chain(c, step, True)

            @pl.when(jnp.logical_not(z_first(c)))
            def _():
                chain(c, step, False)
        return stage

    def chain_end(c):
        own[c, z] = z_total(c, True).astype(BF)
        remote(own.at[c, z, 1 - xh], xr2.at[c], x2_send, x2_recv.at[c], partner, t).start()

    def add_partner(c):
        wait_bytes(xr.at[c], x_recv.at[c])
        own[c, :, xh] = (own[c, :, xh].astype(F32) + xr[c].astype(F32)).astype(BF)

    def z_direct(c):
        add_partner(c)

        def send(j, carry):
            zz = lax.rem(z + j, 8)
            remote(own.at[c, zz, xh], zr.at[c, j - 1], z_send, z_recv.at[c, 0], zz * 2 + xh, t).start()
            return carry

        lax.fori_loop(1, 8, send, 0)

    def activate(c, total):
        gate, up = total[:, 0:256], total[:, 256:512]
        hs[c] = (gate / (1.0 + jnp.exp(-gate)) * up).astype(BF)

    def hidden(c):
        @pl.when(z_first(c))
        def _():
            wait_bytes(xr2.at[c], x2_recv.at[c])
            activate(c, own[c, z, xh].astype(F32) + xr2[c].astype(F32))

        @pl.when(jnp.logical_not(among(c, ZFIRST + DIRECT)))
        def _():
            activate(c, z_total(c, False))

        @pl.when(among(c, DIRECT))
        def _():
            wait_bytes(zr.at[c], z_recv.at[c, 0])
            total = own[c, z, xh].astype(F32)
            for j in range(7):
                total = total + zr[c, j].astype(F32)
            activate(c, total)

        send_hidden(c)

    def send_hidden(c):
        @pl.when(t == c)
        def _():
            w1r[t] = hs[c]

        @pl.when(t != c)
        def _():
            remote(hs.at[c], w1r.at[t], w1_send, w1_recv, d, c).start()

    def mix(c):
        @pl.when(t == c)
        def _():
            wait_bytes(w1r.at[pl.ds(0, NT - 1)], w1_recv)
            turned = jnp.dot(w1r[...].reshape(256, 256), perm_h[...], preferred_element_type=F32).astype(BF)
            mixed = jnp.dot(walsh[...], turned, preferred_element_type=F32) * (1.0 / math.sqrt(FF))
            v[...] = mixed.astype(BF).reshape(16, 16, 256)
            g[c, z, xh] = v[t]

            def send(j, carry):
                to = lax.rem(t + j, NT)
                remote(v.at[to], g.at[c, z, xh], w2_send, w2_recv.at[c], d, to).start()
                return carry

            lax.fori_loop(1, NT, send, 0)

    def wait_mixed(b):
        @pl.when(t != b)
        def _():
            wait_bytes(g.at[b, z, xh], w2_recv.at[b])

    def gather_all(b):
        wait_mixed(b)

        def send(j, carry):
            part = g.at[b, z, xh]
            remote(part, part, gl_send.at[b], g_recv.at[b], lax.rem(d + j, NDP), t).start()
            return carry

        lax.fori_loop(1, NDP, send, 0)

    def gather_z(b):
        wait_mixed(b)

        def send(j, carry):
            zz = lax.rem(z + j, 8)
            remote(g.at[b, z, xh], g.at[b, z, xh], g_send, g_recv.at[b], zz * 2 + xh, t).start()
            return carry

        lax.fori_loop(1, 8, send, 0)

    def gather_x(b):
        wait_bytes(g.at[b, pl.ds(0, 7), xh], g_recv.at[b])
        half = g.at[b, :, xh]
        remote(half, half, gx_send, gx_recv.at[b], partner, t).start()

    def turn(b):
        @pl.when(jnp.logical_not(among(b, WIDE)))
        def _():
            wait_bytes(g.at[b, :, 1 - xh], gx_recv.at[b])

        @pl.when(among(b, WIDE))
        def _():
            wait_bytes(v.at[pl.ds(0, NDP - 1)], g_recv.at[b])

        unpack(b)
        left = g[b].reshape(256, 256)
        for n in range(NB):
            cols = slice(256 * n, 256 * n + 256)
            racc[:, cols] += jnp.dot(left, st[:, cols], preferred_element_type=F32)

    def aside(b):
        @pl.when(b < NB)
        def _():
            down_weights(b)

        @pl.when(b == 13)
        def _():
            share_words()

        @pl.when(b == 14)
        def _():
            words_to_sibling()

        @pl.when(b == 15)
        def _():
            words_of(1, s3_sem.at[1])

    stages = (gate_up, chain_start, chain_on(2), chain_on(3), chain_on(4), chain_end, z_direct, hidden, mix, gather_z,
              gather_x, turn, gather_all, aside)
    def three(i, carry):
        codes = jnp.int32(0)
        for k, number in enumerate(ORDER):
            codes = jnp.where(i == k, number, codes)

        def one(j, codes):
            code = lax.rem(codes, 256)
            block = lax.rem(code, 16)
            for k, stage in enumerate(stages):
                @pl.when(code // 16 == k)
                def _():
                    stage(block)
            return codes // 256

        lax.fori_loop(0, 3, one, codes)
        return carry

    lax.fori_loop(0, len(ORDER), three, 0)

    rot[...] = racc[...].astype(BF).reshape(16, 16, HB)
    top = jnp.max(jnp.abs(rot[d].astype(F32)), axis=1, keepdims=True)
    pk[...] = jnp.broadcast_to(top, (16, 128))
    pr[t] = pk[...]

    def send_peak(j, carry):
        remote(pk, pr.at[t], p_send, p_recv, d, lax.rem(t + j, NT)).start()
        return carry

    lax.fori_loop(1, NT, send_peak, 0)

    width = 1024 // NOUT
    for n in range(NOUT):
        cols = slice(width * n, width * n + width)
        part = jnp.dot(rot[...].reshape(256, HB), dw[:, cols], preferred_element_type=F32)
        es[n] = part.astype(BF).reshape(16, 16, width)
        er[n, t] = es[n, t]

        def send_out(j, carry, n=n):
            to = lax.rem(t + j, NT)
            remote(es.at[n, to], er.at[n, t], e_send.at[n], e_recv.at[n], d, to).start()
            return carry

        lax.fori_loop(1, NT, send_out, 0)

    wait_bytes(pr.at[pl.ds(0, NT - 1)], p_recv)
    high = pr[0]
    for q in range(1, NT):
        high = jnp.maximum(high, pr[q])
    peak[...] = jnp.transpose(high)[0:1, :]

    for n in range(NOUT):
        wait_bytes(er.at[n, pl.ds(0, NT - 1)], e_recv.at[n])
        total = er[n, 0].astype(F32)
        for q in range(1, NT):
            total = total + er[n, q].astype(F32)
        total = total.astype(BF)
        for m in range(width // 256):
            lo = width * n + 256 * m
            out[:, lo:lo + 256] = jnp.dot(
                total[:, 256 * m:256 * m + 256], perm_out[...], preferred_element_type=F32).astype(BF)

    wait_bytes(x.at[core, pl.ds(0, NDP - 1)], a_send)
    sib.wait_send()

    @pl.when(s < 7)
    def _():
        wait_bytes(sw.at[pl.ds(0, 2), pl.ds(0, NDP - 1)], s1_send)
        wait_bytes(sw.at[pl.ds(0, 6)], s2_send)

    words_of(0, s3_sem.at[0])
    wait_bytes(xr.at[pl.ds(0, NB - NZF)], x_send)
    wait_bytes(zr.at[pl.ds(0, NB - NZF)], z_send)
    for b in WIDE:
        wait_bytes(v.at[pl.ds(0, NDP - 1)], gl_send.at[b])
    if NZF:
        wait_bytes(xr2.at[pl.ds(0, NZF)], x2_send)
        wait_bytes(zr2.at[pl.ds(0, NZF)], zz_send)

    @pl.when(t < NB)
    def _():
        wait_bytes(hs.at[pl.ds(0, NB - 1)], w1_send)
        wait_bytes(v.at[pl.ds(0, NT - 1)], w2_send)

    @pl.when(t >= NB)
    def _():
        wait_bytes(hs, w1_send)

    wait_bytes(g.at[pl.ds(0, NB - len(WIDE)), pl.ds(0, 7), 0], g_send)
    wait_bytes(g.at[pl.ds(0, NB - len(WIDE)), :, 0], gx_send)
    for n in range(NOUT):
        wait_bytes(es.at[n, pl.ds(0, NT - 1)], e_send.at[n])
    wait_bytes(pr.at[pl.ds(0, NT - 1)], p_send)


def local(tokens, gc, gs, uc, us, dc, ds, sb):
    dma = pltpu.SemaphoreType.DMA
    vm = pltpu.VMEM
    any_spec = pl.BlockSpec(memory_space=pl.ANY)
    vm_spec = pl.BlockSpec(memory_space=pltpu.VMEM)
    width = 1024 // NOUT
    out, peak = pl.pallas_call(
        body,
        out_shape=(jax.ShapeDtypeStruct((16, 1024), BF), jax.ShapeDtypeStruct((1, 16), F32)),
        in_specs=[any_spec, any_spec, vm_spec, any_spec, vm_spec, any_spec, vm_spec, vm_spec],
        out_specs=(vm_spec, vm_spec),
        scratch_shapes=[
            vm((2, 16, 16, 512), BF),
            vm((NB, 1024, 128), BF),
            vm((NB, 1024, 128), BF),
            vm((HB, 512), BF),
            vm((NB, 8, 2, 16, 512), BF),
            vm((NB, 8, 16, 512), BF),
            vm((NB, 7, 16, 512), BF),
            vm((NB, 7, 2, 16, 512), BF),
            vm((NB, 16, 512), BF),
            vm((NB, 16, 256), BF),
            vm((16, 16, 256), BF),
            vm((16, 16, 256), BF),
            vm((NB, 8, 2, 16, 256), BF),
            vm((14, 16, 16, 256), jnp.int16),
            vm((256, HB), BF),
            vm((HB, 1024), BF),
            vm((256, HB), F32),
            vm((16, 16, HB), BF),
            vm((NOUT, 16, 16, width), BF),
            vm((NOUT, 16, 16, width), BF),
            vm((16, 128), F32),
            vm((16, 16, 128), F32),
            vm((NB, 8, 256), F32),
            vm((NB, 8, 256), F32),
            vm((26, 1024), F32),
            vm((256, 256), jnp.int32),
            vm((16, 16, 256), jnp.int32),
            vm((1024, 512), BF),
            vm((256, 256), BF),
            vm((256, 256), BF),
            vm((256, 256), BF),
            vm((256, 256), BF),
            dma((2, NB)), dma, dma, dma, dma, dma((2,)), dma, dma, dma, dma((4,)),
            dma((2,)), dma, dma((NB,)), dma, dma((NB,)), dma, dma((NB, 7)), dma, dma((NB, 7)), dma((NB,)), dma, dma, dma, dma((NB,)), dma, dma((NB,)),
            dma, dma((NB,)), dma((NOUT,)), dma((NOUT,)), dma, dma,
        ],
        compiler_params=pltpu.CompilerParams(
            collective_id=0, has_side_effects=True, vmem_limit_bytes=63 * 1024 * 1024),
    )(tokens, gc, gs, uc, us, dc, ds, sb)

    def hand_on(a, b, c, e, sems):
        copies = (pltpu.make_async_copy(a, c, sems.at[0]), pltpu.make_async_copy(b, e, sems.at[1]))
        for copy in copies:
            copy.start()
        for copy in copies:
            copy.wait()

    out, peak = pl.pallas_call(
        hand_on, out_shape=(jax.ShapeDtypeStruct((16, 1024), BF), jax.ShapeDtypeStruct((1, 16), F32)),
        in_specs=[any_spec, any_spec], out_specs=(any_spec, any_spec), scratch_shapes=[dma((2,))],
        compiler_params=pltpu.CompilerParams(vmem_limit_bytes=63 * 1024 * 1024))(out, peak)
    return out, peak.reshape(16)


def solution(mesh):
    return jax.shard_map(
        local,
        mesh=mesh,
        in_specs=(
            P("dp", None),
            P("dp", "tensor"),
            P("dp", "tensor"),
            P("dp", "tensor"),
            P("dp", "tensor"),
            P("tensor", "dp"),
            P("tensor", "dp"),
            P("dp", None),
        ),
        out_specs=(P("tensor", "dp"), P("dp")),
        check_vma=False,
    )
```

```python
import functools
import math

import jax
import jax.numpy as jnp
from jax import lax
from jax.experimental import pallas as pl
from jax.experimental.pallas import tpu as pltpu
from jax.sharding import PartitionSpec as P

FF = 53248
HB = 3328
NB = 13
NDP = 16
NT = 16
MESH = pl.DeviceIdType.MESH
BF = jnp.bfloat16
F32 = jnp.float32

ZFIRST = (0, 1, 3, 4, 6, 8, 11)
DIRECT = ()
WIDE = (12,)
NZF = len(ZFIRST)
ORDER = (131328, 318723, 401413, 2295585, 599048, 1232944, 3221002, 3345361, 2627026, 13841420, 1516096, 4314166, 2442027, 13973529, 3297348, 1714134, 3887430, 5496535, 2742325, 7358492, 3621460, 5647065, 4541297, 14301555, 7493676, 7620480, 7789370, 5993857, 3965769, 7895004, 8669826, 8812944, 5012357, 8033169, 9603207, 9010324, 9803403, 9931424, 9214113, 10197411, 11591586, 11639460, 11783334, 10990245, 11118772, 11905974, 12105642, 12303545, 16777146)

NOUT = 2


def among(c, blocks):
    return functools.reduce(jnp.logical_or, [c == k for k in blocks], c < 0)


def eo_column(p):
    return jnp.where(p < 128, 2 * p, 2 * (p - 128) + 1)


def one_hot(cond):
    return jnp.where(cond, 1.0, 0.0).astype(BF)


def body(tokens, gc, gs, uc, us, dc, ds, sb, out, peak,
         x, gcv, ucv, dcv, own, xr, zr, zr2, xr2, hs, w1r, v, g, sw, st, dw, racc, rot, es, er, pk, pr,
         gsv, usv, dsv, sbp, sbt, wb, perm_in, perm_h, perm_out, walsh,
         code_sem, dcode_sem, loc_sem, a_send, a_recv, sib_sem, s1_send, s1_recv, s2_send, s2_recv,
         s3_sem, x_send, x_recv, x2_send, x2_recv, z_send, z_recv, zz_send, zz_recv, gl_send, w1_send, w1_recv, w2_send, w2_recv, g_send, g_recv,
         gx_send, gx_recv, e_send, e_recv, p_send, p_recv):
    d = lax.axis_index("dp")
    t = lax.axis_index("tensor")
    core = lax.rem(t, 2)
    y = lax.rem(t // 2, 4)
    s = core * 4 + y
    z = d // 2
    xh = lax.rem(d, 2)
    partner = z * 2 + (1 - xh)
    sibling = t + 1 - 2 * core

    def remote(src, dst, ssem, rsem, dp, tn):
        return pltpu.make_async_remote_copy(
            src_ref=src, dst_ref=dst, send_sem=ssem, recv_sem=rsem, device_id=(dp, tn), device_id_type=MESH)

    def wait_bytes(ref, sem):
        pltpu.make_async_copy(ref, ref, sem).wait()

    barrier = pltpu.get_barrier_semaphore()

    def greet(j, carry):
        pl.semaphore_signal(barrier, inc=1, device_id=(lax.rem(d + j, NDP), t), device_id_type=MESH)
        pl.semaphore_signal(barrier, inc=1, device_id=(d, lax.rem(t + j, NT)), device_id_type=MESH)
        return carry

    lax.fori_loop(1, NDP, greet, 0)

    def code_copies(c):
        lanes = pl.ds(pl.multiple_of(c * 128, 128), 128)
        return (pltpu.make_async_copy(gc.at[:, lanes], gcv.at[c], code_sem.at[0, c]),
                pltpu.make_async_copy(uc.at[:, lanes], ucv.at[c], code_sem.at[1, c]))

    def start_codes(c, carry):
        for copy in code_copies(c):
            copy.start()
        return carry

    lax.fori_loop(0, NB, start_codes, 0)
    dcopy = pltpu.make_async_copy(dc, dcv, dcode_sem)
    dcopy.start()

    sbp[...] = jnp.zeros_like(sbp)
    sbp[0:208, 0:208] = sb[...]
    sbt[...] = jnp.transpose(sbp[...]).reshape(16, 16, 256)

    @pl.when(s < 7)
    def _():
        for u in range(2):
            sw[2 * s + u, d] = sbt[2 * s + u].astype(jnp.int16)

    pl.semaphore_wait(barrier, 2 * (NDP - 1))

    def token_copy(dst_dp):
        lanes = pl.ds(pl.multiple_of(dst_dp * 1024 + core * 512, 512), 512)
        return tokens.at[:, lanes]

    def send_tokens(j, carry):
        to = lax.rem(d + 1 + lax.rem(j + 5, NDP - 1), NDP)
        remote(token_copy(to), x.at[core, d], a_send, a_recv, to, t).start()
        return carry

    lax.fori_loop(1, NDP, send_tokens, 0)
    mine = pltpu.make_async_copy(token_copy(d), x.at[core, d], loc_sem)
    mine.start()

    @pl.when(s < 7)
    def _():
        def send_words(j, carry):
            part = sw.at[pl.ds(2 * s, 2), d]
            remote(part, part, s1_send, s1_recv, lax.rem(d + j, NDP), t).start()
            return carry

        lax.fori_loop(1, NDP, send_words, 0)

    src = lax.broadcasted_iota(jnp.int32, (256, 256), 0)
    dst = lax.broadcasted_iota(jnp.int32, (256, 256), 1)
    perm_in[...] = one_hot(src == eo_column(dst))
    perm_out[...] = one_hot(dst == eo_column(src))
    perm_h[...] = one_hot(eo_column(src) == 16 * (dst & 15) + (dst >> 4))
    both = (src >> 4) & (dst >> 4)
    odd = (both ^ (both >> 1) ^ (both >> 2) ^ (both >> 3)) & 1
    walsh[...] = jnp.where((src & 15) == (dst & 15), jnp.where(odd == 1, -1.0, 1.0), 0.0).astype(BF)

    racc[...] = jnp.zeros_like(racc)

    for b in range(NB):
        cols = slice(256 * b, 256 * b + 256)
        gsv[b] = jnp.dot(gs[:, cols], perm_in[...], preferred_element_type=F32)
        usv[b] = jnp.dot(us[:, cols], perm_in[...], preferred_element_type=F32)
    for n in range(4):
        cols = slice(256 * n, 256 * n + 256)
        dsv[:, cols] = jnp.dot(ds[:, cols], perm_in[...], preferred_element_type=F32)

    wait_bytes(x.at[core, pl.ds(0, NDP - 1)], a_recv)
    mine.wait()
    sib = remote(x.at[core], x.at[core], sib_sem.at[0], sib_sem.at[1], d, sibling)
    sib.start()
    sib.wait_recv()

    def nibbles(codes):
        whole = codes.astype(F32)
        high = jnp.floor(whole * 0.0625)
        return whole - 16.0 * high - 8.0, high - 8.0

    def gate_up(c):
        for copy in code_copies(c):
            copy.wait()
        for base, codes, scales in ((0, gcv, gsv), (256, ucv, usv)):
            for r in range(8):
                rows = slice(128 * r, 128 * r + 128)
                low, high = nibbles(codes[c, rows, :])
                sc = scales[c, r:r + 1, :]
                wb[rows, base:base + 128] = (low * sc[:, 0:128]).astype(BF)
                wb[rows, base + 128:base + 256] = (high * sc[:, 128:256]).astype(BF)
        part = jnp.dot(x[0].reshape(256, 512), wb[0:512, :], preferred_element_type=F32)
        part = part + jnp.dot(x[1].reshape(256, 512), wb[512:1024, :], preferred_element_type=F32)
        own[c] = part.astype(BF).reshape(8, 2, 16, 512)

        @pl.when(z_first(c))
        def _():
            chain(c, 1, True)

        @pl.when(jnp.logical_not(z_first(c)))
        def _():
            remote(own.at[c, :, 1 - xh], xr.at[c], x_send, x_recv.at[c], partner, t).start()

    def down_weights(b):
        @pl.when(b == 0)
        def _():
            dcopy.wait()

        for r in range(2):
            rows = pl.ds(pl.multiple_of(256 * b + 128 * r, 128), 128)
            low, high = nibbles(dcv[rows, :])
            sc = dsv[pl.ds(2 * b + r, 1), :]
            for n in range(4):
                words = slice(128 * n, 128 * n + 128)
                dw[rows, 256 * n:256 * n + 128] = (low[:, words] * sc[:, 256 * n:256 * n + 128]).astype(BF)
                dw[rows, 256 * n + 128:256 * n + 256] = (high[:, words] * sc[:, 256 * n + 128:256 * n + 256]).astype(BF)

    def share_words():
        @pl.when(s < 7)
        def _():
            wait_bytes(sw.at[pl.ds(0, 2), pl.ds(0, NDP - 1)], s1_recv)

            def send(j, carry):
                to = t + 2 * (lax.rem(y + j, 4) - y)
                part = sw.at[pl.ds(2 * s, 2)]
                remote(part, part, s2_send, s2_recv.at[y], d, to).start()
                return carry

            lax.fori_loop(1, 4, send, 0)

    def words_to_sibling():
        for q in range(4):
            @pl.when((y != q) & (core * 4 + q < 7))
            def _():
                wait_bytes(sw.at[pl.ds(2 * q, 2)], s2_recv.at[q])

        @pl.when(core == 0)
        def _():
            remote(sw.at[pl.ds(0, 8)], sw.at[pl.ds(0, 8)], s3_sem.at[0], s3_sem.at[1], d, sibling).start()

        @pl.when(core == 1)
        def _():
            remote(sw.at[pl.ds(8, 6)], sw.at[pl.ds(8, 6)], s3_sem.at[0], s3_sem.at[1], d, sibling).start()

    def words_of(which, sem):
        @pl.when(core == which)
        def _():
            wait_bytes(sw.at[pl.ds(0, 8)], sem)

        @pl.when(core != which)
        def _():
            wait_bytes(sw.at[pl.ds(8, 6)], sem)

    def unpack(b):
        words = jnp.concatenate([sw[b, q].astype(jnp.int32)[:, 0:208] for q in range(NDP)], axis=1)
        for k in range(16):
            st[16 * k:16 * k + 16, :] = jnp.where((words & (1 << k)) == 0, 1.0, -1.0).astype(BF)

    def z_first(c):
        return among(c, ZFIRST)

    def chain(c, step, first):
        sign = 1 - 2 * lax.rem(c, 2)
        buf, ss, rs, m = (zr2, zz_send, zz_recv, c) if first else (zr, z_send, z_recv, c)
        for way, base, steps in ((1, 0, 4), (-1, 4, 3)):
            if step > steps:
                continue
            owner = lax.rem(z + way * sign * (steps + 1 - step) + 8, 8)
            term = own.at[c, owner] if first else own.at[c, owner, xh]
            if step > 1:
                src = buf.at[m, base + step - 2]
                wait_bytes(src, rs.at[m, base + step - 2])
                src[...] = (src[...].astype(F32) + term[...].astype(F32)).astype(BF)
            else:
                src = term
            to = lax.rem(z + way * sign + 8, 8) * 2 + xh
            remote(src, buf.at[m, base + step - 1], ss, rs.at[m, base + step - 1], to, t).start()

    def z_total(c, first):
        buf, rs, m = (zr2, zz_recv, c) if first else (zr, z_recv, c)
        term = own[c, z] if first else own[c, z, xh]
        wait_bytes(buf.at[m, 3], rs.at[m, 3])
        wait_bytes(buf.at[m, 6], rs.at[m, 6])
        return term.astype(F32) + buf[m, 3].astype(F32) + buf[m, 6].astype(F32)

    def chain_start(c):
        add_partner(c)
        chain(c, 1, False)

    def chain_on(step):
        def stage(c):
            @pl.when(z_first(c))
            def _():
                chain(c, step, True)

            @pl.when(jnp.logical_not(z_first(c)))
            def _():
                chain(c, step, False)
        return stage

    def chain_end(c):
        own[c, z] = z_total(c, True).astype(BF)
        remote(own.at[c, z, 1 - xh], xr2.at[c], x2_send, x2_recv.at[c], partner, t).start()

    def add_partner(c):
        wait_bytes(xr.at[c], x_recv.at[c])
        own[c, :, xh] = (own[c, :, xh].astype(F32) + xr[c].astype(F32)).astype(BF)

    def z_direct(c):
        add_partner(c)

        def send(j, carry):
            zz = lax.rem(z + j, 8)
            remote(own.at[c, zz, xh], zr.at[c, j - 1], z_send, z_recv.at[c, 0], zz * 2 + xh, t).start()
            return carry

        lax.fori_loop(1, 8, send, 0)

    def activate(c, total):
        gate, up = total[:, 0:256], total[:, 256:512]
        hs[c] = (gate / (1.0 + jnp.exp(-gate)) * up).astype(BF)

    def hidden(c):
        @pl.when(z_first(c))
        def _():
            wait_bytes(xr2.at[c], x2_recv.at[c])
            activate(c, own[c, z, xh].astype(F32) + xr2[c].astype(F32))

        @pl.when(jnp.logical_not(among(c, ZFIRST + DIRECT)))
        def _():
            activate(c, z_total(c, False))

        @pl.when(among(c, DIRECT))
        def _():
            wait_bytes(zr.at[c], z_recv.at[c, 0])
            total = own[c, z, xh].astype(F32)
            for j in range(7):
                total = total + zr[c, j].astype(F32)
            activate(c, total)

        send_hidden(c)

    def send_hidden(c):
        @pl.when(t == c)
        def _():
            w1r[t] = hs[c]

        @pl.when(t != c)
        def _():
            remote(hs.at[c], w1r.at[t], w1_send, w1_recv, d, c).start()

    def mix(c):
        @pl.when(t == c)
        def _():
            wait_bytes(w1r.at[pl.ds(0, NT - 1)], w1_recv)
            turned = jnp.dot(w1r[...].reshape(256, 256), perm_h[...], preferred_element_type=F32).astype(BF)
            mixed = jnp.dot(walsh[...], turned, preferred_element_type=F32) * (1.0 / math.sqrt(FF))
            v[...] = mixed.astype(BF).reshape(16, 16, 256)
            g[c, z, xh] = v[t]

            def send(j, carry):
                to = lax.rem(t + j, NT)
                remote(v.at[to], g.at[c, z, xh], w2_send, w2_recv.at[c], d, to).start()
                return carry

            lax.fori_loop(1, NT, send, 0)

    def wait_mixed(b):
        @pl.when(t != b)
        def _():
            wait_bytes(g.at[b, z, xh], w2_recv.at[b])

    def gather_all(b):
        wait_mixed(b)

        def send(j, carry):
            part = g.at[b, z, xh]
            remote(part, part, gl_send.at[b], g_recv.at[b], lax.rem(d + j, NDP), t).start()
            return carry

        lax.fori_loop(1, NDP, send, 0)

    def gather_z(b):
        wait_mixed(b)

        def send(j, carry):
            zz = lax.rem(z + j, 8)
            remote(g.at[b, z, xh], g.at[b, z, xh], g_send, g_recv.at[b], zz * 2 + xh, t).start()
            return carry

        lax.fori_loop(1, 8, send, 0)

    def gather_x(b):
        wait_bytes(g.at[b, pl.ds(0, 7), xh], g_recv.at[b])
        half = g.at[b, :, xh]
        remote(half, half, gx_send, gx_recv.at[b], partner, t).start()

    def turn(b):
        @pl.when(jnp.logical_not(among(b, WIDE)))
        def _():
            wait_bytes(g.at[b, :, 1 - xh], gx_recv.at[b])

        @pl.when(among(b, WIDE))
        def _():
            wait_bytes(v.at[pl.ds(0, NDP - 1)], g_recv.at[b])

        unpack(b)
        left = g[b].reshape(256, 256)
        for n in range(NB):
            cols = slice(256 * n, 256 * n + 256)
            racc[:, cols] += jnp.dot(left, st[:, cols], preferred_element_type=F32)

    def aside(b):
        @pl.when(b < NB)
        def _():
            down_weights(b)

        @pl.when(b == 13)
        def _():
            share_words()

        @pl.when(b == 14)
        def _():
            words_to_sibling()

        @pl.when(b == 15)
        def _():
            words_of(1, s3_sem.at[1])

    stages = (gate_up, chain_start, chain_on(2), chain_on(3), chain_on(4), chain_end, z_direct, hidden, mix, gather_z,
              gather_x, turn, gather_all, aside)
    def three(i, carry):
        codes = jnp.int32(0)
        for k, number in enumerate(ORDER):
            codes = jnp.where(i == k, number, codes)

        def one(j, codes):
            code = lax.rem(codes, 256)
            block = lax.rem(code, 16)
            for k, stage in enumerate(stages):
                @pl.when(code // 16 == k)
                def _():
                    stage(block)
            return codes // 256

        lax.fori_loop(0, 3, one, codes)
        return carry

    lax.fori_loop(0, len(ORDER), three, 0)

    rot[...] = racc[...].astype(BF).reshape(16, 16, HB)
    top = jnp.max(jnp.abs(rot[d].astype(F32)), axis=1, keepdims=True)
    pk[...] = jnp.broadcast_to(top, (16, 128))
    pr[t] = pk[...]

    def send_peak(j, carry):
        remote(pk, pr.at[t], p_send, p_recv, d, lax.rem(t + j, NT)).start()
        return carry

    lax.fori_loop(1, NT, send_peak, 0)

    width = 1024 // NOUT
    for n in range(NOUT):
        cols = slice(width * n, width * n + width)
        part = jnp.dot(rot[...].reshape(256, HB), dw[:, cols], preferred_element_type=F32)
        es[n] = part.astype(BF).reshape(16, 16, width)
        er[n, t] = es[n, t]

        def send_out(j, carry, n=n):
            to = lax.rem(t + j, NT)
            remote(es.at[n, to], er.at[n, t], e_send.at[n], e_recv.at[n], d, to).start()
            return carry

        lax.fori_loop(1, NT, send_out, 0)

    wait_bytes(pr.at[pl.ds(0, NT - 1)], p_recv)
    high = pr[0]
    for q in range(1, NT):
        high = jnp.maximum(high, pr[q])
    peak[...] = jnp.transpose(high)[0:1, :]

    for n in range(NOUT):
        wait_bytes(er.at[n, pl.ds(0, NT - 1)], e_recv.at[n])
        total = er[n, 0].astype(F32)
        for q in range(1, NT):
            total = total + er[n, q].astype(F32)
        total = total.astype(BF)
        for m in range(width // 256):
            lo = width * n + 256 * m
            out[:, lo:lo + 256] = jnp.dot(
                total[:, 256 * m:256 * m + 256], perm_out[...], preferred_element_type=F32).astype(BF)

    wait_bytes(x.at[core, pl.ds(0, NDP - 1)], a_send)
    sib.wait_send()

    @pl.when(s < 7)
    def _():
        wait_bytes(sw.at[pl.ds(0, 2), pl.ds(0, NDP - 1)], s1_send)
        wait_bytes(sw.at[pl.ds(0, 6)], s2_send)

    words_of(0, s3_sem.at[0])
    wait_bytes(xr.at[pl.ds(0, NB - NZF)], x_send)
    wait_bytes(zr.at[pl.ds(0, NB - NZF)], z_send)
    for b in WIDE:
        wait_bytes(v.at[pl.ds(0, NDP - 1)], gl_send.at[b])
    if NZF:
        wait_bytes(xr2.at[pl.ds(0, NZF)], x2_send)
        wait_bytes(zr2.at[pl.ds(0, NZF)], zz_send)

    @pl.when(t < NB)
    def _():
        wait_bytes(hs.at[pl.ds(0, NB - 1)], w1_send)
        wait_bytes(v.at[pl.ds(0, NT - 1)], w2_send)

    @pl.when(t >= NB)
    def _():
        wait_bytes(hs, w1_send)

    wait_bytes(g.at[pl.ds(0, NB - len(WIDE)), pl.ds(0, 7), 0], g_send)
    wait_bytes(g.at[pl.ds(0, NB - len(WIDE)), :, 0], gx_send)
    for n in range(NOUT):
        wait_bytes(es.at[n, pl.ds(0, NT - 1)], e_send.at[n])
    wait_bytes(pr.at[pl.ds(0, NT - 1)], p_send)


def local(tokens, gc, gs, uc, us, dc, ds, sb):
    dma = pltpu.SemaphoreType.DMA
    vm = pltpu.VMEM
    any_spec = pl.BlockSpec(memory_space=pl.ANY)
    vm_spec = pl.BlockSpec(memory_space=pltpu.VMEM)
    width = 1024 // NOUT
    out, peak = pl.pallas_call(
        body,
        out_shape=(jax.ShapeDtypeStruct((16, 1024), BF), jax.ShapeDtypeStruct((1, 16), F32)),
        in_specs=[any_spec, any_spec, vm_spec, any_spec, vm_spec, any_spec, vm_spec, vm_spec],
        out_specs=(vm_spec, vm_spec),
        scratch_shapes=[
            vm((2, 16, 16, 512), BF),
            vm((NB, 1024, 128), BF),
            vm((NB, 1024, 128), BF),
            vm((HB, 512), BF),
            vm((NB, 8, 2, 16, 512), BF),
            vm((NB, 8, 16, 512), BF),
            vm((NB, 7, 16, 512), BF),
            vm((NB, 7, 2, 16, 512), BF),
            vm((NB, 16, 512), BF),
            vm((NB, 16, 256), BF),
            vm((16, 16, 256), BF),
            vm((16, 16, 256), BF),
            vm((NB, 8, 2, 16, 256), BF),
            vm((14, 16, 16, 256), jnp.int16),
            vm((256, HB), BF),
            vm((HB, 1024), BF),
            vm((256, HB), F32),
            vm((16, 16, HB), BF),
            vm((NOUT, 16, 16, width), BF),
            vm((NOUT, 16, 16, width), BF),
            vm((16, 128), F32),
            vm((16, 16, 128), F32),
            vm((NB, 8, 256), F32),
            vm((NB, 8, 256), F32),
            vm((26, 1024), F32),
            vm((256, 256), jnp.int32),
            vm((16, 16, 256), jnp.int32),
            vm((1024, 512), BF),
            vm((256, 256), BF),
            vm((256, 256), BF),
            vm((256, 256), BF),
            vm((256, 256), BF),
            dma((2, NB)), dma, dma, dma, dma, dma((2,)), dma, dma, dma, dma((4,)),
            dma((2,)), dma, dma((NB,)), dma, dma((NB,)), dma, dma((NB, 7)), dma, dma((NB, 7)), dma((NB,)), dma, dma, dma, dma((NB,)), dma, dma((NB,)),
            dma, dma((NB,)), dma((NOUT,)), dma((NOUT,)), dma, dma,
        ],
        compiler_params=pltpu.CompilerParams(
            collective_id=0, has_side_effects=True, vmem_limit_bytes=63 * 1024 * 1024),
    )(tokens, gc, gs, uc, us, dc, ds, sb)

    def hand_on(a, b, c, e, sems):
        copies = (pltpu.make_async_copy(a, c, sems.at[0]), pltpu.make_async_copy(b, e, sems.at[1]))
        for copy in copies:
            copy.start()
        for copy in copies:
            copy.wait()

    out, peak = pl.pallas_call(
        hand_on, out_shape=(jax.ShapeDtypeStruct((16, 1024), BF), jax.ShapeDtypeStruct((1, 16), F32)),
        in_specs=[any_spec, any_spec], out_specs=(any_spec, any_spec), scratch_shapes=[dma((2,))],
        compiler_params=pltpu.CompilerParams(vmem_limit_bytes=63 * 1024 * 1024))(out, peak)
    return out, peak.reshape(16)


def solution(mesh):
    return jax.shard_map(
        local,
        mesh=mesh,
        in_specs=(
            P("dp", None),
            P("dp", "tensor"),
            P("dp", "tensor"),
            P("dp", "tensor"),
            P("dp", "tensor"),
            P("tensor", "dp"),
            P("tensor", "dp"),
            P("dp", None),
        ),
        out_specs=(P("tensor", "dp"), P("dp")),
        check_vma=False,
    )
```
